32 devices in a mesh: row: 4 (over y, core), col: 8 (over z, x).
Axes of the slice: x: 2, y: 2, z: 4, core: 2. Of those that a mesh axis runs over, the one named last changes fastest.
Arguments:
- params: float32 [64, 8192], replicated, may hold values from -6 to 6
- momentum: float32 [4, 8, 64, 8192], P('row', 'col'), may hold values from -6 to 6
- gradient: float32 [4, 8, 64, 8192], P('row', 'col'), may hold values from -6 to 6
- chosen_rows: int32 [4, 8, 128, 4], P('row', 'col'), may hold values from 0 to 63, as said below
- live_counts: int32 [4, 8, 128], P('row', 'col'), may hold values from 1 to 4, as said below
- common_rows: int32 [8, 128, 8], P('col'), may hold values from 0 to 63, as said below
Outputs:
- new_params: float32 [64, 8192], replicated
- new_momentum: float32 [4, 8, 64, 8192], P('row', 'col')
The draws below stay inside these ranges and needn't reach their ends.
Inputs may be any that keep to these rules, and one draw needn't show every extreme that they name: `chosen_rows`: within one replica's block the 4 entries are distinct; entries at positions at or past the block's live count are ignored. `live_counts`: every replica has 4 live rows in some block. `common_rows`: within one group's block the 8 entries are distinct.
All inputs are finite; a program needn't handle non-finite values.
Results may differ from the reference program's by a relative error of at most 0.0003.
Values sent between devices are 32-bit elements; how exact they have to be, the bound alone decides.
No kernel may reach another device: no remote copies, remote signals or barrier semaphores. Data moves between devices by JAX's collectives and lax.ppermute only.
A program may use at most 128 MiB of HBM per device.

```python
import math
import jax
import jax.numpy as jnp
from jax import lax

CH = 64
SPANS = 128
S = 4
Q = 8
W = 8192
N_ROW = 4
N_COL = 8


def order_table(key):
    keys = jax.random.split(jax.random.fold_in(key, 11), N_COL * SPANS)
    orders = jax.vmap(lambda single: jax.random.permutation(single, CH))(keys)
    return orders.reshape(N_COL, SPANS, CH).astype(jnp.int32)


def draw_common_rows(key, part):
    return order_table(key)[:, :, :Q]


def draw_chosen_rows(key, part):
    orders = order_table(key)
    keys = jax.random.split(jax.random.fold_in(key, 23), N_ROW * N_COL * SPANS)
    places = jax.vmap(lambda single: jax.random.permutation(single, 2 * Q)[:S])(keys)
    places = places.reshape(N_ROW, N_COL, SPANS, S).astype(jnp.int32)
    wide = jnp.broadcast_to(orders[None], (N_ROW, N_COL, SPANS, CH))
    return jnp.take_along_axis(wide, places, axis=3).astype(jnp.int32)


def draw_live_counts(key, part):
    counts = jax.random.randint(jax.random.fold_in(key, 31), (N_ROW, N_COL, SPANS), 1, S + 1)
    return counts.at[:, :, 0].set(S).astype(jnp.int32)


def block_scale(key, dims, pieces, low, top_value):
    def one(dim, shards_of):
        steps = jax.random.uniform(jax.random.fold_in(jax.random.fold_in(key, 6), dim), (shards_of,), jnp.float32, low / len(pieces), top_value / len(pieces))
        return jnp.repeat(jnp.exp(steps), dims[dim] // shards_of).reshape((-1,) + (1,) * (len(dims) - dim - 1))

    gain = one(*pieces[0])
    for cut in pieces[1:]:
        gain = gain * one(*cut)
    return gain


def centred(own_key, shape, scale, limit, cuts=(), kind=jnp.bfloat16):
    entries = scale * jax.random.normal(own_key, shape, jnp.float32)
    if cuts:
        entries = entries * block_scale(own_key, shape, cuts, -0.22, 0.18)
    return jnp.clip(entries, -limit, limit).astype(kind)


def setup_inputs(seed: int = 0) -> dict:
    key_list = jax.random.split(jax.random.key(seed), 7)
    params = centred(key_list[0], (CH, W), 1.0, 6.0, (), jnp.float32)
    momentum = centred(key_list[1], (N_ROW, N_COL, CH, W), 1.0, 6.0, ((0, 4), (1, 8)), jnp.float32)
    gradient = centred(key_list[2], (N_ROW, N_COL, CH, W), 1.0, 6.0, ((0, 4), (1, 8)), jnp.float32)
    chosen_rows = draw_chosen_rows(jax.random.fold_in(key_list[6], 71), 0)
    live_counts = draw_live_counts(jax.random.fold_in(key_list[6], 71), 0)
    common_rows = draw_common_rows(jax.random.fold_in(key_list[6], 71), 0)
    return {"params": params, "momentum": momentum, "gradient": gradient, "chosen_rows": chosen_rows, "live_counts": live_counts, "common_rows": common_rows}


decay_rate = 0.9
step_size = 0.1
highest = lax.Precision.HIGHEST

def dct_table(order):
    freq = jnp.arange(order, dtype=jnp.float32)[:, None]
    place = jnp.arange(order, dtype=jnp.float32)[None, :]
    matrix = math.sqrt(2.0 / order) * jnp.cos(math.pi * (2.0 * place + 1.0) * freq / (2.0 * order))
    return jnp.where(freq == 0.0, matrix * math.sqrt(0.5), matrix)

def block_pair(matrix):
    return jnp.kron(jnp.eye(2, dtype=jnp.float32), matrix)

def forward(field):
    matrix = dct_table(CH)
    across = jnp.dot(matrix, field, precision=highest, preferred_element_type=jnp.float32)
    shaped = across.reshape(-1, 2 * CH)
    result = jnp.dot(shaped, block_pair(matrix.T), precision=highest, preferred_element_type=jnp.float32)
    return result.reshape(field.shape)

def inverse(field):
    matrix = dct_table(CH)
    across = jnp.dot(matrix.T, field, precision=highest, preferred_element_type=jnp.float32)
    shaped = across.reshape(-1, 2 * CH)
    result = jnp.dot(shaped, block_pair(matrix), precision=highest, preferred_element_type=jnp.float32)
    return result.reshape(field.shape)

def pick_table(chosen, counts):
    table = (chosen[..., None] == jnp.arange(CH, dtype=jnp.int32)).astype(jnp.float32)
    if counts is not None:
        live = (jnp.arange(chosen.shape[-1], dtype=jnp.int32) < counts[..., None]).astype(jnp.float32)
        table = table * live[..., None]
    return table

def local_step(item):
    moment, grads, chosen, counts = item
    decayed = decay_rate * moment + grads
    spectrum = forward(decayed)
    cube = spectrum.reshape(CH, SPANS, CH)
    picked = pick_table(chosen, counts)
    values = jnp.einsum('ksf,fkg->ksg', picked, cube, precision=highest)
    sent = jnp.einsum('ksf,ksg->fkg', picked, values, precision=highest)
    residual = decayed - inverse(sent.reshape(CH, -1))
    return (residual, sent)

def reference(params, momentum, gradient, chosen_rows, live_counts, common_rows):

    def group_step(column):
        items = (momentum[:, column], gradient[:, column], chosen_rows[:, column], live_counts[:, column])
        residuals, sents = lax.map(local_step, items)
        summed = lax.optimization_barrier(jnp.sum(sents, axis=0))
        cut_table = pick_table(common_rows[column], None)
        kept = jnp.einsum('kqf,fkg->kqg', cut_table, summed, precision=highest)
        spread = jnp.einsum('kqf,kqg->fkg', cut_table, kept, precision=highest)
        return (residuals, spread)
    residuals, spreads = lax.map(group_step, jnp.arange(N_COL, dtype=jnp.int32))
    total = lax.optimization_barrier(jnp.sum(spreads, axis=0))
    new_params = params - step_size * inverse(total.reshape(CH, -1))
    new_momentum = jnp.transpose(residuals, (1, 0, 2, 3))
    return (new_params, new_momentum)
```

```python
import functools
import math

import jax
import jax.numpy as jnp
import ml_dtypes
import numpy as np
from jax import lax
from jax.experimental import pallas as pl
from jax.experimental.pallas import tpu as pltpu
from jax.sharding import PartitionSpec as P

decay_rate = 0.9
step_size = 0.1
LANES = 128
SUB = 8
CORES = 2
EVERY = ("row", "col")
VMEM_BYTES = 48 * 1024 * 1024


def dct_table(order):
    freq = np.arange(order, dtype=np.float64)[:, None]
    place = np.arange(order, dtype=np.float64)[None, :]
    matrix = math.sqrt(2.0 / order) * np.cos(math.pi * (2.0 * place + 1.0) * freq / (2.0 * order))
    return np.where(freq == 0.0, matrix * math.sqrt(0.5), matrix)


def split_table(matrix):
    high = matrix.astype(ml_dtypes.bfloat16)
    low = (matrix - high.astype(np.float64)).astype(ml_dtypes.bfloat16)
    return np.concatenate([high, low, high], axis=1)


def product(table, field):
    high = field.astype(jnp.bfloat16)
    low = (field - high.astype(jnp.float32)).astype(jnp.bfloat16)
    stacked = jnp.concatenate([high, high, low], axis=0)
    return jnp.dot(table, stacked, preferred_element_type=jnp.float32)


def lane_blocks(order, first):
    return first + lax.broadcasted_iota(jnp.int32, (SUB, LANES), 1) // order


def pick_kernel(width, table_ref, chosen_ref, counts_ref, common_ref, m_ref, g_ref, out_ref):
    order = m_ref.shape[-2]
    chosen = chosen_ref[...]
    common = common_ref[...]
    slot = lax.broadcasted_iota(jnp.int32, chosen.shape, 0)
    inside = chosen == common[0:1]
    for q in range(1, common.shape[0]):
        inside = inside | (chosen == common[q : q + 1])
    rows = jnp.where(inside & (slot < counts_ref[...]), chosen, -1)
    rows = jnp.concatenate([rows, rows], axis=0)
    slots = chosen.shape[0]
    spectrum = product(table_ref[...], decay_rate * m_ref[0, 0] + g_ref[0, 0])
    step_blocks = m_ref.shape[-1] // order
    first = lax.rem(pl.program_id(0) * step_blocks, LANES)
    values_part = lax.broadcasted_iota(jnp.int32, (SUB, LANES), 0) < slots
    for t in range(m_ref.shape[-1] // LANES):
        lanes = lane_blocks(order, first + t * (LANES // order))
        row = jnp.take_along_axis(rows, lanes, axis=1)
        tile, within = row >> 3, row & 7
        picked = jnp.zeros((SUB, LANES), jnp.float32)
        for r in range(order // SUB):
            here = spectrum[r * SUB : (r + 1) * SUB, t * LANES : (t + 1) * LANES]
            picked = jnp.where(tile == r, jnp.take_along_axis(here, within, axis=0), picked)
        column = t * LANES
        out_ref[column // width, :, column % width : column % width + LANES] = jnp.where(
            values_part, picked, row.astype(jnp.float32)
        )


def rest_kernel(table_ref, back_ref, chosen_ref, counts_ref, m_ref, g_ref, out_ref):
    order, columns = m_ref.shape[-2:]
    chosen = chosen_ref[...]
    slot = lax.broadcasted_iota(jnp.int32, chosen.shape, 0)
    bits = jnp.where(slot < counts_ref[...], jnp.int32(1) << (chosen & 31), 0)
    words = []
    for half in range(order // 32):
        mine = jnp.where((chosen >> 5) == half, bits, 0)
        word = mine[0:1]
        for s in range(1, chosen.shape[0]):
            word = word | mine[s : s + 1]
        words.append(jnp.broadcast_to(word, (SUB, LANES)))
    decayed = decay_rate * m_ref[0, 0] + g_ref[0, 0]
    spectrum = product(table_ref[...], decayed)
    first = lax.rem(pl.program_id(0) * (columns // order), LANES)
    sub = lax.broadcasted_iota(jnp.int32, (SUB, LANES), 0)
    parts = []
    for t in range(columns // LANES):
        lanes = lane_blocks(order, first + t * (LANES // order))
        wide = [jnp.take_along_axis(word, lanes, axis=1) for word in words]
        tiles = []
        for r in range(order // SUB):
            here = spectrum[r * SUB : (r + 1) * SUB, t * LANES : (t + 1) * LANES]
            bit = jnp.int32(1) << (sub + (r * SUB) % 32)
            tiles.append(jnp.where((wide[r * SUB // 32] & bit) != 0, here, 0.0))
        parts.append(jnp.concatenate(tiles, axis=0))
    sent = jnp.concatenate(parts, axis=1)
    out_ref[0, 0] = decayed - product(back_ref[...], sent)


def sum_kernel(back_ref, got_ref, params_ref, out_ref, held, arrived):
    order, width = out_ref.shape
    me = lax.axis_index("row") * lax.axis_size("col") + lax.axis_index("col")
    copy = pltpu.make_async_copy(
        params_ref.at[:, pl.ds(pl.multiple_of(me * width, LANES), width)], held, arrived
    )
    copy.start()
    slots = got_ref.shape[1] // 2
    tiles = order // SUB
    sub = lax.broadcasted_iota(jnp.int32, (SUB, LANES), 0).astype(jnp.float32)

    def add(n, totals):
        totals = list(totals)
        for t in range(width // LANES):
            got = got_ref[n, :, t * LANES : (t + 1) * LANES]
            for s in range(slots):
                value = jnp.broadcast_to(got[s : s + 1], (SUB, LANES))
                row = jnp.broadcast_to(got[slots + s : slots + s + 1], (SUB, LANES)) - sub
                for r in range(tiles):
                    k = t * tiles + r
                    totals[k] = totals[k] + jnp.where(row == r * SUB, value, 0.0)
        return tuple(totals)

    zero = jnp.zeros((SUB, LANES), jnp.float32)
    totals = lax.fori_loop(0, got_ref.shape[0], add, (zero,) * (tiles * (width // LANES)))
    total = jnp.concatenate(
        [
            jnp.concatenate(totals[t * tiles : (t + 1) * tiles], axis=0)
            for t in range(width // LANES)
        ],
        axis=1,
    )
    update = product(back_ref[...], total)
    copy.wait()
    out_ref[...] = held[...] - step_size * update


def place_kernel(places, sizes, *refs):
    *pieces, out_ref, sems = refs
    y_size, z_size, x_size = sizes
    row, col = lax.axis_index("row"), lax.axis_index("col")
    y, core, z, x = row // CORES, row % CORES, col // x_size, col % x_size
    copies = []
    for piece, (other, first, second) in zip(pieces, places, strict=True):
        owner = 1 - core if other else core
        dy = jnp.where(owner == 0, first, second)
        dx = jnp.where(owner == 0, second, first)
        width = piece.shape[-1]
        for j in range(z_size):
            place = ((y ^ dy) * CORES + owner) * (z_size * x_size) + (z ^ j) * x_size + (x ^ dx)
            copy = pltpu.make_async_copy(
                piece.at[j],
                out_ref.at[:, pl.ds(pl.multiple_of(place * width, LANES), width)],
                sems.at[len(copies)],
            )
            copy.start()
            copies.append(copy)
    for copy in copies:
        copy.wait()


def vmem():
    return pl.BlockSpec(memory_space=pltpu.VMEM)


def limits():
    return pltpu.CompilerParams(vmem_limit_bytes=VMEM_BYTES)


def list_spec(rows, step):
    return pl.BlockSpec((rows, LANES), lambda i: (0, i * step // LANES))


def pick(forward, momentum, gradient, chosen, counts, common, parts):
    order, columns = momentum.shape[-2:]
    width = columns // parts
    step = max(width, columns // 8)
    lists = functools.partial(list_spec, step=step // order)
    field = pl.BlockSpec((1, 1, order, step), lambda i: (0, 0, 0, i))
    slots = chosen.shape[0]
    return pl.pallas_call(
        functools.partial(pick_kernel, width),
        grid=(columns // step,),
        in_specs=[vmem(), lists(slots), lists(1), lists(common.shape[0]), field, field],
        out_specs=pl.BlockSpec((step // width, 2 * slots, width), lambda i: (i, 0, 0)),
        out_shape=jax.ShapeDtypeStruct((parts, 2 * slots, width), jnp.float32),
        compiler_params=limits(),
        name="pick_rows",
    )(forward, chosen, counts, common, momentum, gradient)


def rest(forward, back, momentum, gradient, chosen, counts):
    order, columns = momentum.shape[-2:]
    step = columns // 8
    lists = functools.partial(list_spec, step=step // order)
    field = pl.BlockSpec((1, 1, order, step), lambda i: (0, 0, 0, i))
    return pl.pallas_call(
        rest_kernel,
        grid=(columns // step,),
        in_specs=[vmem(), vmem(), lists(chosen.shape[0]), lists(1), field, field],
        out_specs=field,
        out_shape=jax.ShapeDtypeStruct(momentum.shape, jnp.float32),
        compiler_params=limits(),
        name="residual",
        cost_estimate=pl.CostEstimate(
            flops=12 * order * order * columns,
            bytes_accessed=3 * momentum.size * 4,
            transcendentals=0,
        ),
    )(forward, back, chosen, counts, momentum, gradient)


def add_up(back, got, params):
    width = got.shape[-1]
    order = params.shape[0]
    return pl.pallas_call(
        sum_kernel,
        in_specs=[vmem(), vmem(), pl.BlockSpec(memory_space=pl.ANY)],
        out_specs=vmem(),
        out_shape=jax.ShapeDtypeStruct((order, width), jnp.float32),
        scratch_shapes=[pltpu.VMEM((order, width), jnp.float32), pltpu.SemaphoreType.DMA],
        compiler_params=limits(),
        name="sum_and_update",
    )(back, got, params)


def spread(mine, sizes):
    y_size, z_size, x_size = sizes

    def swap(array, zero, one):
        pairs = []
        for y in range(y_size):
            for core in range(CORES):
                for z in range(z_size):
                    for x in range(x_size):
                        dy, dk, dz, dx = (zero, one)[core]
                        here = ((y * CORES + core) * z_size + z) * x_size + x
                        there = (((y ^ dy) * CORES + (core ^ dk)) * z_size + (z ^ dz)) * x_size + (
                            x ^ dx
                        )
                        pairs.append((here, there))
        return lax.ppermute(array, EVERY, pairs)

    line = [mine] + [swap(mine, (0, 0, j, 0), (0, 0, j, 0)) for j in range(1, z_size)]
    own = jnp.stack(line)
    pieces = [(own, 0, 0)]
    first = []
    for i in range(1, x_size):
        got = swap(own, (0, 0, 0, i), (i, 0, 0, 0))
        first.append((got, 0, i))
    pieces += first
    for j in range(1, y_size):
        pieces.append((swap(own, (j, 0, 0, 0), (0, 0, 0, j)), j, 0))
        for array, _, i in first:
            pieces.append((swap(array, (j, 0, 0, 0), (0, 0, 0, j)), j, i))
    other = [(swap(array, (0, 1, 0, 0), (0, 1, 0, 0)), dy, dx) for array, dy, dx in pieces]
    return [(array, 0, dy, dx) for array, dy, dx in pieces] + [
        (array, 1, dy, dx) for array, dy, dx in other
    ]


def place(pieces, sizes, params):
    arrays = [piece[0] for piece in pieces]
    places = [piece[1:] for piece in pieces]
    anywhere = pl.BlockSpec(memory_space=pl.ANY)
    return pl.pallas_call(
        functools.partial(place_kernel, places, sizes),
        in_specs=[anywhere] * len(arrays),
        out_specs=anywhere,
        out_shape=jax.ShapeDtypeStruct(params.shape, jnp.float32),
        scratch_shapes=[pltpu.SemaphoreType.DMA((len(arrays) * sizes[1],))],
        compiler_params=limits(),
        name="place_columns",
    )(*arrays)


def body(sizes, parts, params, momentum, gradient, chosen_rows, live_counts, common_rows):
    matrix = dct_table(params.shape[0])
    forward, back = jnp.asarray(split_table(matrix)), jnp.asarray(split_table(matrix.T))
    chosen = jnp.transpose(chosen_rows[0, 0])
    counts = live_counts[0]
    common = jnp.transpose(common_rows[0])
    sent = pick(forward, momentum, gradient, chosen, counts, common, parts)
    residual = rest(forward, back, momentum, gradient, chosen, counts)
    if sizes is not None:
        got = lax.all_to_all(sent, EVERY, 0, 0, tiled=True)
        mine = add_up(back, got, params)
        new_params = place(spread(mine, sizes), sizes, params)
    else:
        new_params = plain_update(back, sent, params)
    return new_params, residual


def plain_update(back, sent, params):
    order, columns = params.shape
    got = lax.all_to_all(sent, "col", 0, 0, tiled=True)
    got = lax.all_gather(got, "row", axis=0, tiled=True)
    slots = sent.shape[1] // 2
    row = got[:, slots:].astype(jnp.int32)
    table = row[:, :, None, :] == jnp.arange(order, dtype=jnp.int32)[:, None]
    total = jnp.sum(jnp.where(table, got[:, :slots, None, :], 0.0), axis=(0, 1))
    total = lax.all_gather(total, "col", axis=1, tiled=True)
    return params - step_size * product(back, total)


def solution(mesh):
    rows, cols = mesh.shape["row"], mesh.shape["col"]
    placed = (
        P(),
        P("row", "col", None, None),
        P("row", "col", None, None),
        P("row", "col", None, None),
        P("row", "col", None),
        P("col", None, None),
    )

    def step(params, *rest_of):
        columns = params.shape[1]
        side = rows // CORES
        depth = cols // max(side, 1)
        whole = rows == side * CORES and cols == side * depth
        powers = all(n > 0 and n & (n - 1) == 0 for n in (side, depth))
        shared = columns % (rows * cols * LANES) == 0
        sizes = (side, depth, side) if whole and powers and shared else None
        parts = cols if sizes is None else rows * cols
        return jax.shard_map(
            functools.partial(body, sizes, parts),
            mesh=mesh,
            in_specs=placed,
            out_specs=(P(), P("row", "col", None, None)),
            check_vma=False,
        )(params, *rest_of)

    return step
```

```python
import functools
import math

import jax
import jax.numpy as jnp
import ml_dtypes
import numpy as np
from jax import lax
from jax.experimental import pallas as pl
from jax.experimental.pallas import tpu as pltpu
from jax.sharding import PartitionSpec as P

decay_rate = 0.9
step_size = 0.1
LANES = 128
SUB = 8
CORES = 2
EVERY = ("row", "col")
VMEM_BYTES = 48 * 1024 * 1024


def dct_table(order):
    freq = np.arange(order, dtype=np.float64)[:, None]
    place = np.arange(order, dtype=np.float64)[None, :]
    matrix = math.sqrt(2.0 / order) * np.cos(math.pi * (2.0 * place + 1.0) * freq / (2.0 * order))
    return np.where(freq == 0.0, matrix * math.sqrt(0.5), matrix)


def split_table(matrix):
    high = matrix.astype(ml_dtypes.bfloat16)
    low = (matrix - high.astype(np.float64)).astype(ml_dtypes.bfloat16)
    return np.concatenate([high, low, high], axis=1)


def product(table, field):
    high = field.astype(jnp.bfloat16)
    low = (field - high.astype(jnp.float32)).astype(jnp.bfloat16)
    stacked = jnp.concatenate([high, high, low], axis=0)
    return jnp.dot(table, stacked, preferred_element_type=jnp.float32)


def lane_blocks(order, first):
    return first + lax.broadcasted_iota(jnp.int32, (SUB, LANES), 1) // order


def pick_kernel(width, steps, *refs):
    sources, out_ref, held, arrived = refs[:6], refs[6], refs[7:13], refs[13]
    table_ref, chosen_ref, counts_ref, common_ref, m_ref, g_ref = held
    order, columns = m_ref.shape
    step = columns // steps
    copies = [
        pltpu.make_async_copy(source, target, arrived.at[n])
        for n, (source, target) in enumerate(zip(sources[:4], held[:4], strict=True))
    ]
    for i in range(steps):
        cut = pl.ds(i * step, step)
        for source, target in zip(sources[4:], held[4:], strict=True):
            copies.append(
                pltpu.make_async_copy(
                    source.at[0, 0, :, cut], target.at[:, cut], arrived.at[len(copies)]
                )
            )
    for copy in copies:
        copy.start()
    for copy in copies[:4]:
        copy.wait()
    chosen = chosen_ref[...]
    common = common_ref[...]
    slots = chosen.shape[0]
    slot = lax.broadcasted_iota(jnp.int32, chosen.shape, 0)
    inside = chosen == common[0:1]
    for q in range(1, common.shape[0]):
        inside = inside | (chosen == common[q : q + 1])
    rows = jnp.where(inside & (slot < counts_ref[...]), chosen, -1)
    rows = jnp.concatenate([rows, rows], axis=0)
    share = width // order
    for i in range(steps):
        for copy in copies[4 + 2 * i : 6 + 2 * i]:
            copy.wait()
        cut = pl.ds(i * step, step)
        spectrum = product(table_ref[...], decay_rate * m_ref[:, cut] + g_ref[:, cut])
        for t in range(step // LANES):
            column = i * step + t * LANES
            part, at = divmod(column, width)
            row = block_lanes(rows, order, column // order)
            tile, within = row >> 3, row & 7
            picked = jnp.zeros((SUB, LANES), jnp.float32)
            for r in range(order // SUB):
                here = spectrum[r * SUB : (r + 1) * SUB, t * LANES : (t + 1) * LANES]
                picked = jnp.where(
                    tile == r, jnp.take_along_axis(here, within, axis=0), picked
                )
            out_ref[part, :, at : at + LANES] = picked[:slots]
            if at == 0:
                lanes = lax.broadcasted_iota(jnp.int32, (SUB, LANES), 1)
                lanes = column // order + jnp.minimum(lanes, share - 1)
                numbers = take_blocks(rows, lanes, column // order)
                out_ref[part, :, width : width + LANES] = numbers[:slots].astype(jnp.float32)


def take_blocks(rows, lanes, first):
    base = first // LANES * LANES
    return jnp.take_along_axis(rows[:, base : base + LANES], lanes - base, axis=1)


def block_lanes(rows, order, first):
    lanes = first + lax.broadcasted_iota(jnp.int32, (SUB, LANES), 1) // order
    return take_blocks(rows, lanes, first)


def rest_kernel(table_ref, back_ref, chosen_ref, counts_ref, m_ref, g_ref, out_ref):
    order, columns = m_ref.shape[-2:]
    chosen = chosen_ref[...]
    slot = lax.broadcasted_iota(jnp.int32, chosen.shape, 0)
    bits = jnp.where(slot < counts_ref[...], jnp.int32(1) << (chosen & 31), 0)
    words = []
    for half in range(order // 32):
        mine = jnp.where((chosen >> 5) == half, bits, 0)
        word = mine[0:1]
        for s in range(1, chosen.shape[0]):
            word = word | mine[s : s + 1]
        words.append(jnp.broadcast_to(word, (SUB, LANES)))
    decayed = decay_rate * m_ref[0, 0] + g_ref[0, 0]
    spectrum = product(table_ref[...], decayed)
    first = lax.rem(pl.program_id(0) * (columns // order), LANES)
    sub = lax.broadcasted_iota(jnp.int32, (SUB, LANES), 0)
    parts = []
    for t in range(columns // LANES):
        lanes = lane_blocks(order, first + t * (LANES // order))
        wide = [jnp.take_along_axis(word, lanes, axis=1) for word in words]
        tiles = []
        for r in range(order // SUB):
            here = spectrum[r * SUB : (r + 1) * SUB, t * LANES : (t + 1) * LANES]
            bit = jnp.int32(1) << (sub + (r * SUB) % 32)
            tiles.append(jnp.where((wide[r * SUB // 32] & bit) != 0, here, 0.0))
        parts.append(jnp.concatenate(tiles, axis=0))
    sent = jnp.concatenate(parts, axis=1)
    out_ref[0, 0] = decayed - product(back_ref[...], sent)


def sum_kernel(back_ref, got_ref, params_ref, out_ref, held, arrived):
    order, width = out_ref.shape
    me = lax.axis_index("row") * lax.axis_size("col") + lax.axis_index("col")
    copy = pltpu.make_async_copy(
        params_ref.at[:, pl.ds(pl.multiple_of(me * width, LANES), width)], held, arrived
    )
    copy.start()
    slots = got_ref.shape[1]
    tiles = order // SUB
    sub = lax.broadcasted_iota(jnp.int32, (SUB, LANES), 0).astype(jnp.float32)

    def add(n, totals):
        totals = list(totals)
        numbers = jnp.concatenate([got_ref[n, :, width:]] * 2, axis=0)
        for t in range(width // LANES):
            values = got_ref[n, :, t * LANES : (t + 1) * LANES]
            rows = block_lanes(numbers, order, t * (LANES // order))
            for s in range(slots):
                value = jnp.broadcast_to(values[s : s + 1], (SUB, LANES))
                row = jnp.broadcast_to(rows[s : s + 1], (SUB, LANES)) - sub
                for r in range(tiles):
                    k = t * tiles + r
                    totals[k] = totals[k] + jnp.where(row == r * SUB, value, 0.0)
        return tuple(totals)

    zero = jnp.zeros((SUB, LANES), jnp.float32)
    totals = lax.fori_loop(
        0, got_ref.shape[0], add, (zero,) * (tiles * (width // LANES)), unroll=8
    )
    total = jnp.concatenate(
        [
            jnp.concatenate(totals[t * tiles : (t + 1) * tiles], axis=0)
            for t in range(width // LANES)
        ],
        axis=1,
    )
    update = product(back_ref[...], total)
    copy.wait()
    out_ref[...] = held[...] - step_size * update


def place_kernel(places, sizes, *refs):
    *pieces, out_ref, sems = refs
    y_size, z_size, x_size = sizes
    row, col = lax.axis_index("row"), lax.axis_index("col")
    y, core, z, x = row // CORES, row % CORES, col // x_size, col % x_size
    copies = []
    for piece, (other, dy, dx) in zip(pieces, places, strict=True):
        owner = 1 - core if other else core
        width = piece.shape[-1]
        for j in range(z_size):
            place = ((y ^ dy) * CORES + owner) * (z_size * x_size) + (z ^ j) * x_size + (x ^ dx)
            copy = pltpu.make_async_copy(
                piece.at[j],
                out_ref.at[:, pl.ds(pl.multiple_of(place * width, LANES), width)],
                sems.at[len(copies)],
            )
            copy.start()
            copies.append(copy)
    for copy in copies:
        copy.wait()


def in_hbm(array):
    return pltpu.with_memory_space_constraint(array, pltpu.HBM)


def vmem():
    return pl.BlockSpec(memory_space=pltpu.VMEM)


def limits():
    return pltpu.CompilerParams(vmem_limit_bytes=VMEM_BYTES)


def list_spec(rows, step):
    return pl.BlockSpec((rows, LANES), lambda i: (0, i * step // LANES))


def pick(forward, momentum, gradient, chosen, counts, common, parts):
    order, columns = momentum.shape[-2:]
    width = columns // parts
    steps = min(8, parts)
    slots = chosen.shape[0]
    sources = (forward, chosen, counts, common, momentum, gradient)
    held = [pltpu.VMEM(source.shape[-2:], source.dtype) for source in sources]
    return pl.pallas_call(
        functools.partial(pick_kernel, width, steps),
        in_specs=[pl.BlockSpec(memory_space=pltpu.HBM)] * len(sources),
        out_specs=vmem(),
        out_shape=jax.ShapeDtypeStruct((parts, slots, width + LANES), jnp.float32),
        scratch_shapes=held + [pltpu.SemaphoreType.DMA((4 + 2 * steps,))],
        compiler_params=limits(),
        name="pick_rows",
    )(*map(in_hbm, sources))


def rest(forward, back, momentum, gradient, chosen, counts):
    order, columns = momentum.shape[-2:]
    step = columns // 8
    lists = functools.partial(list_spec, step=step // order)
    field = pl.BlockSpec((1, 1, order, step), lambda i: (0, 0, 0, i))
    return pl.pallas_call(
        rest_kernel,
        grid=(columns // step,),
        in_specs=[vmem(), vmem(), lists(chosen.shape[0]), lists(1), field, field],
        out_specs=field,
        out_shape=jax.ShapeDtypeStruct(momentum.shape, jnp.float32),
        compiler_params=limits(),
        name="residual",
        cost_estimate=pl.CostEstimate(
            flops=12 * order * order * columns,
            bytes_accessed=3 * momentum.size * 4,
            transcendentals=0,
        ),
    )(forward, back, chosen, counts, momentum, gradient)


def add_up(back, got, params):
    width = got.shape[-1] - LANES
    order = params.shape[0]
    return pl.pallas_call(
        sum_kernel,
        in_specs=[vmem(), vmem(), pl.BlockSpec(memory_space=pltpu.HBM)],
        out_specs=vmem(),
        out_shape=jax.ShapeDtypeStruct((order, width), jnp.float32),
        scratch_shapes=[pltpu.VMEM((order, width), jnp.float32), pltpu.SemaphoreType.DMA],
        compiler_params=limits(),
        name="sum_and_update",
    )(back, got, in_hbm(params))


def spread(mine, residual, sizes):
    y_size, z_size, x_size = sizes

    def swap(array, by):
        pairs = []
        for y in range(y_size):
            for core in range(CORES):
                for z in range(z_size):
                    for x in range(x_size):
                        here = ((y * CORES + core) * z_size + z) * x_size + x
                        there = ((y ^ by[0]) * CORES + (core ^ by[1])) * z_size + (z ^ by[2])
                        pairs.append((here, there * x_size + (x ^ by[3])))
        return lax.ppermute(array, EVERY, pairs)

    line = [mine] + [swap(mine, (0, 0, j, 0)) for j in range(1, z_size)]
    own = jnp.stack(line)
    far = [(j, i) for j in range(y_size) for i in range(x_size) if j or i]
    far.sort(key=lambda at: sum(map(bool, at)))
    pieces = [(own, 0, 0)] + [(swap(own, (j, 0, 0, i)), j, i) for j, i in far]
    others = [(swap(array, (0, 1, 0, 0)), j, i) for array, j, i in pieces[:-1]]
    array, j, i = pieces.pop()
    array, residual, early = lax.optimization_barrier((array, residual, [o[0] for o in others]))
    pieces.append((array, j, i))
    others = [(a, o[1], o[2]) for a, o in zip(early, others, strict=True)]
    others.append((swap(array, (0, 1, 0, 0)), j, i))
    return pieces, others, residual


def place(pieces, sizes, params):
    arrays = [piece[0] for piece in pieces]
    places = [piece[1:] for piece in pieces]
    anywhere = pl.BlockSpec(memory_space=pl.ANY)
    return pl.pallas_call(
        functools.partial(place_kernel, places, sizes),
        in_specs=[anywhere] * len(arrays),
        out_specs=anywhere,
        out_shape=jax.ShapeDtypeStruct(params.shape, jnp.float32),
        scratch_shapes=[pltpu.SemaphoreType.DMA((len(arrays) * sizes[1],))],
        compiler_params=limits(),
        name="place_columns",
    )(*arrays)


def body(sizes, parts, params, momentum, gradient, chosen_rows, live_counts, common_rows):
    matrix = dct_table(params.shape[0])
    forward, back = jnp.asarray(split_table(matrix)), jnp.asarray(split_table(matrix.T))
    chosen = jnp.transpose(chosen_rows[0, 0])
    counts = live_counts[0]
    common = jnp.transpose(common_rows[0])
    sent = pick(forward, momentum, gradient, chosen, counts, common, parts)
    residual = rest(forward, back, momentum, gradient, chosen, counts)
    if sizes is not None:
        got = lax.all_to_all(sent, EVERY, 0, 0, tiled=True)
        mine = add_up(back, got, params)
        near, others, residual = spread(mine, residual, sizes)
        pieces = [(a, 0, j, i) for a, j, i in near] + [(a, 1, j, i) for a, j, i in others]
        new_params = place(pieces, sizes, params)
    else:
        new_params = plain_update(back, sent, params)
    return new_params, residual


def plain_update(back, sent, params):
    order, columns = params.shape
    got = lax.all_to_all(sent, "col", 0, 0, tiled=True)
    got = lax.all_gather(got, "row", axis=0, tiled=True)
    width = columns // sent.shape[0]
    row = got[:, :, width : width + width // order].astype(jnp.int32)
    row = jnp.repeat(row, order, axis=2)
    table = row[:, :, None, :] == jnp.arange(order, dtype=jnp.int32)[:, None]
    total = jnp.sum(jnp.where(table, got[:, :, None, :width], 0.0), axis=(0, 1))
    total = lax.all_gather(total, "col", axis=1, tiled=True)
    return params - step_size * product(back, total)


def solution(mesh):
    rows, cols = mesh.shape["row"], mesh.shape["col"]
    placed = (
        P(),
        P("row", "col", None, None),
        P("row", "col", None, None),
        P("row", "col", None, None),
        P("row", "col", None),
        P("col", None, None),
    )

    def step(params, *rest_of):
        columns = params.shape[1]
        side = rows // CORES
        depth = cols // max(side, 1)
        whole = rows == side * CORES and cols == side * depth
        powers = all(n > 0 and n & (n - 1) == 0 for n in (side, depth))
        shared = columns % (rows * cols * LANES) == 0
        sizes = (side, depth, side) if whole and powers and shared else None
        parts = cols if sizes is None else rows * cols
        return jax.shard_map(
            functools.partial(body, sizes, parts),
            mesh=mesh,
            in_specs=placed,
            out_specs=(P(), P("row", "col", None, None)),
            check_vma=False,
        )(params, *rest_of)

    return step
```

```python
import functools
import math

import jax
import jax.numpy as jnp
import ml_dtypes
import numpy as np
from jax import lax
from jax.experimental import pallas as pl
from jax.experimental.pallas import tpu as pltpu
from jax.sharding import PartitionSpec as P

decay_rate = 0.9
step_size = 0.1
LANES = 128
SUB = 8
CORES = 2
EVERY = ("row", "col")
VMEM_BYTES = 48 * 1024 * 1024
LATE = (0, 3)


def dct_table(order):
    freq = np.arange(order, dtype=np.float64)[:, None]
    place = np.arange(order, dtype=np.float64)[None, :]
    matrix = math.sqrt(2.0 / order) * np.cos(math.pi * (2.0 * place + 1.0) * freq / (2.0 * order))
    return np.where(freq == 0.0, matrix * math.sqrt(0.5), matrix)


def split_table(matrix):
    high = matrix.astype(ml_dtypes.bfloat16)
    low = (matrix - high.astype(np.float64)).astype(ml_dtypes.bfloat16)
    return np.concatenate([high, low, high], axis=1)


def product(table, field):
    high = field.astype(jnp.bfloat16)
    low = (field - high.astype(jnp.float32)).astype(jnp.bfloat16)
    stacked = jnp.concatenate([high, high, low], axis=0)
    return jnp.dot(table, stacked, preferred_element_type=jnp.float32)


def pick_kernel(width, steps, *refs):
    sources, out_ref, held, arrived = refs[:6], refs[6], refs[7:13], refs[13]
    table_ref, chosen_ref, counts_ref, common_ref, m_ref, g_ref = held
    order, columns = m_ref.shape
    step = columns // steps
    copies = [
        pltpu.make_async_copy(source, target, arrived.at[n])
        for n, (source, target) in enumerate(zip(sources[:4], held[:4], strict=True))
    ]
    for i in range(steps):
        cut = pl.ds(i * step, step)
        for source, target in zip(sources[4:], held[4:], strict=True):
            copies.append(
                pltpu.make_async_copy(
                    source.at[0, 0, :, cut], target.at[:, cut], arrived.at[len(copies)]
                )
            )
    for copy in copies:
        copy.start()
    for copy in copies[:4]:
        copy.wait()
    chosen = chosen_ref[...]
    common = common_ref[...]
    slots = chosen.shape[0]
    slot = lax.broadcasted_iota(jnp.int32, chosen.shape, 0)
    inside = chosen == common[0:1]
    for q in range(1, common.shape[0]):
        inside = inside | (chosen == common[q : q + 1])
    live = jnp.where(slot < counts_ref[...], chosen, -1)
    rows = jnp.where(inside, live, -1)
    live = jnp.concatenate([live, live], axis=0)
    rows = jnp.concatenate([rows, rows], axis=0)
    share = width // order
    for i in range(steps):
        for copy in copies[4 + 2 * i : 6 + 2 * i]:
            copy.wait()
        for part in range(i * step // width, (i + 1) * step // width):
            cut = pl.ds(part * width, width)
            spectrum = product(table_ref[...], decay_rate * m_ref[:, cut] + g_ref[:, cut])
            for t in range(width // LANES):
                row = block_lanes(live, order, (part * width + t * LANES) // order)
                tile, within = row >> 3, row & 7
                picked = jnp.zeros((SUB, LANES), jnp.float32)
                for r in range(order // SUB):
                    here = spectrum[r * SUB : (r + 1) * SUB, t * LANES : (t + 1) * LANES]
                    here = jnp.take_along_axis(here, within, axis=0)
                    picked = jnp.where(tile == r, here, picked)
                out_ref[part, :, t * LANES : (t + 1) * LANES] = picked[:slots]
            lanes = lax.broadcasted_iota(jnp.int32, (SUB, LANES), 1)
            lanes = part * share + jnp.minimum(lanes, share - 1)
            numbers = take_blocks(rows, lanes, part * share)
            out_ref[part, :, width:] = numbers[:slots].astype(jnp.float32)


def take_blocks(rows, lanes, first):
    base = first // LANES * LANES
    return jnp.take_along_axis(rows[:, base : base + LANES], lanes - base, axis=1)


def block_lanes(rows, order, first):
    lanes = first + lax.broadcasted_iota(jnp.int32, (SUB, LANES), 1) // order
    return take_blocks(rows, lanes, first)


def rest_kernel(skipped, start, width, *refs):
    back_ref, chosen_ref, counts_ref, sent_ref, m_ref, g_ref, out_ref, held, gone = refs[skipped:]
    order, columns = held.shape
    chosen = chosen_ref[...]
    slots = chosen.shape[0]
    slot = lax.broadcasted_iota(jnp.int32, chosen.shape, 0)
    live = jnp.where(slot < counts_ref[...], chosen, -1)
    live = jnp.concatenate([live, live], axis=0)
    sub = lax.broadcasted_iota(jnp.int32, (SUB, LANES), 0)
    copies = []
    for part in range(columns // width):
        parts = []
        for t in range(width // LANES):
            values = sent_ref[start + part, :, t * LANES : (t + 1) * LANES]
            rows = block_lanes(live, order, ((start + part) * width + t * LANES) // order)
            wide = [
                (
                    jnp.broadcast_to(rows[s : s + 1], (SUB, LANES)) - sub,
                    jnp.broadcast_to(values[s : s + 1], (SUB, LANES)),
                )
                for s in range(slots)
            ]
            tiles = []
            for r in range(order // SUB):
                tile = jnp.zeros((SUB, LANES), jnp.float32)
                for row, value in wide:
                    tile = jnp.where(row == r * SUB, value, tile)
                tiles.append(tile)
            parts.append(jnp.concatenate(tiles, axis=0))
        back = product(back_ref[...], jnp.concatenate(parts, axis=1))
        cut, here = pl.ds((start + part) * width, width), pl.ds(part * width, width)
        held[:, here] = decay_rate * m_ref[0, 0, :, cut] + g_ref[0, 0, :, cut] - back
        copy = pltpu.make_async_copy(held.at[:, here], out_ref.at[0, 0, :, cut], gone.at[part])
        copy.start()
        copies.append(copy)
    for copy in copies:
        copy.wait()


def sum_kernel(back_ref, got_ref, params_ref, out_ref, held, arrived):
    order, width = out_ref.shape
    me = lax.axis_index("row") * lax.axis_size("col") + lax.axis_index("col")
    copy = pltpu.make_async_copy(
        params_ref.at[:, pl.ds(pl.multiple_of(me * width, LANES), width)], held, arrived
    )
    copy.start()
    slots = got_ref.shape[1]
    tiles = order // SUB
    sub = lax.broadcasted_iota(jnp.int32, (SUB, LANES), 0).astype(jnp.float32)

    def add(n, totals):
        totals = list(totals)
        numbers = jnp.concatenate([got_ref[n, :, width:]] * 2, axis=0)
        for t in range(width // LANES):
            values = got_ref[n, :, t * LANES : (t + 1) * LANES]
            rows = block_lanes(numbers, order, t * (LANES // order))
            for s in range(slots):
                value = jnp.broadcast_to(values[s : s + 1], (SUB, LANES))
                row = jnp.broadcast_to(rows[s : s + 1], (SUB, LANES)) - sub
                for r in range(tiles):
                    k = t * tiles + r
                    totals[k] = totals[k] + jnp.where(row == r * SUB, value, 0.0)
        return tuple(totals)

    zero = jnp.zeros((SUB, LANES), jnp.float32)
    totals = lax.fori_loop(
        0, got_ref.shape[0], add, (zero,) * (tiles * (width // LANES)), unroll=8
    )
    total = jnp.concatenate(
        [
            jnp.concatenate(totals[t * tiles : (t + 1) * tiles], axis=0)
            for t in range(width // LANES)
        ],
        axis=1,
    )
    update = product(back_ref[...], total)
    copy.wait()
    out_ref[...] = held[...] - step_size * update


def place_kernel(places, sizes, skipped, *refs):
    *pieces, out_ref, sems = refs[skipped:]
    y_size, z_size, x_size = sizes
    row, col = lax.axis_index("row"), lax.axis_index("col")
    y, core, z, x = row // CORES, row % CORES, col // x_size, col % x_size
    copies = []
    for piece, (other, dy, dx, dz) in zip(pieces, places, strict=True):
        owner = 1 - core if other else core
        width = piece.shape[-1]
        for j in range(piece.shape[0]):
            place = ((y ^ dy) * CORES + owner) * z_size + (z ^ (dz + j))
            place = place * x_size + (x ^ dx)
            copy = pltpu.make_async_copy(
                piece.at[j],
                out_ref.at[:, pl.ds(pl.multiple_of(place * width, LANES), width)],
                sems.at[len(copies)],
            )
            copy.start()
            copies.append(copy)
    for copy in copies:
        copy.wait()


def in_hbm(array):
    return pltpu.with_memory_space_constraint(array, pltpu.HBM)


def vmem():
    return pl.BlockSpec(memory_space=pltpu.VMEM)


def limits():
    return pltpu.CompilerParams(vmem_limit_bytes=VMEM_BYTES)


def list_spec(rows, step):
    return pl.BlockSpec((rows, LANES), lambda i: (0, i * step // LANES))


def pick(forward, momentum, gradient, chosen, counts, common, parts):
    order, columns = momentum.shape[-2:]
    width = columns // parts
    steps = min(4, parts)
    slots = chosen.shape[0]
    sources = (forward, chosen, counts, common, momentum, gradient)
    held = [pltpu.VMEM(source.shape[-2:], source.dtype) for source in sources]
    return pl.pallas_call(
        functools.partial(pick_kernel, width, steps),
        in_specs=[pl.BlockSpec(memory_space=pltpu.HBM)] * len(sources),
        out_specs=vmem(),
        out_shape=jax.ShapeDtypeStruct((parts, slots, width + LANES), jnp.float32),
        scratch_shapes=held + [pltpu.SemaphoreType.DMA((4 + 2 * steps,))],
        compiler_params=limits(),
        name="pick_rows",
    )(*map(in_hbm, sources))


def rest(back, sent, momentum, gradient, chosen, counts, first, parts, before):
    order = momentum.shape[-2]
    width = sent.shape[-1] - LANES
    anywhere = pl.BlockSpec(memory_space=pl.ANY)
    given = [] if before is None else [before]
    return pl.pallas_call(
        functools.partial(rest_kernel, len(given), first, width),
        in_specs=[anywhere] * len(given) + [vmem()] * 6,
        out_specs=anywhere,
        out_shape=jax.ShapeDtypeStruct(momentum.shape, jnp.float32),
        scratch_shapes=[
            pltpu.VMEM((order, parts * width), jnp.float32),
            pltpu.SemaphoreType.DMA((parts,)),
        ],
        input_output_aliases={0: 0} if given else {},
        compiler_params=limits(),
        name="residual",
        cost_estimate=pl.CostEstimate(
            flops=12 * order * order * momentum.shape[-1] * 100,
            bytes_accessed=3 * momentum.size * 400,
            transcendentals=0,
        ),
    )(*given, back, chosen, counts, sent, momentum, gradient)


def add_up(back, got, params):
    width = got.shape[-1] - LANES
    order = params.shape[0]
    return pl.pallas_call(
        sum_kernel,
        in_specs=[vmem(), vmem(), pl.BlockSpec(memory_space=pltpu.HBM)],
        out_specs=vmem(),
        out_shape=jax.ShapeDtypeStruct((order, width), jnp.float32),
        scratch_shapes=[pltpu.VMEM((order, width), jnp.float32), pltpu.SemaphoreType.DMA],
        compiler_params=limits(),
        name="sum_and_update",
    )(back, got, in_hbm(params))


def spread(mine, piece, params, sizes):
    y_size, z_size, x_size = sizes

    def swap(array, by):
        pairs = []
        for y in range(y_size):
            for core in range(CORES):
                for z in range(z_size):
                    for x in range(x_size):
                        here = ((y * CORES + core) * z_size + z) * x_size + x
                        there = ((y ^ by[0]) * CORES + (core ^ by[1])) * z_size + (z ^ by[2])
                        pairs.append((here, there * x_size + (x ^ by[3])))
        return lax.ppermute(array, EVERY, pairs)

    line = [mine] + [swap(mine, (0, 0, j, 0)) for j in range(1, z_size)]
    far = [(j, i) for j in range(y_size) for i in range(x_size) if j or i]
    far.sort(key=lambda at: sum(map(bool, at)))
    half = max(1, z_size // 2)
    groups = z_size // half
    parts = y_size * CORES * z_size * x_size
    fill = parts // 8
    early, late, residual = [], [], None
    for n in range(groups):
        held = line[n * half : (n + 1) * half]
        if n:
            residual = piece((n - 1) * fill, fill, residual)
            held, residual = lax.optimization_barrier((held, residual))
        own = jnp.stack(held)
        early.append((own, 0, 0, n * half))
        sent = [(swap(own, (j, 0, 0, i)), j, i, n * half) for j, i in far]
        kept = len(sent) - LATE[min(n, 1)]
        early += sent[:kept]
        late += sent[kept:]
    residual = piece((groups - 1) * fill, parts - (groups - 1) * fill, residual)

    def both(array, *at):
        return [(array, 0, *at), (swap(array, (0, 1, 0, 0)), 1, *at)]

    partial = place([made for piece_of in early for made in both(*piece_of)], sizes, params, None)
    arrays = [piece_of[0] for piece_of in late]
    arrays, residual, partial = lax.optimization_barrier((arrays, residual, partial))
    made = [made for array, at in zip(arrays, late, strict=True) for made in both(array, *at[1:])]
    return place(made, sizes, params, partial), residual


def place(pieces, sizes, params, partial):
    arrays = [piece[0] for piece in pieces]
    places = [piece[1:] for piece in pieces]
    anywhere = pl.BlockSpec(memory_space=pl.ANY)
    given = [] if partial is None else [partial]
    return pl.pallas_call(
        functools.partial(place_kernel, places, sizes, len(given)),
        in_specs=[anywhere] * (len(given) + len(arrays)),
        out_specs=anywhere,
        out_shape=jax.ShapeDtypeStruct(params.shape, jnp.float32),
        scratch_shapes=[pltpu.SemaphoreType.DMA((sum(array.shape[0] for array in arrays),))],
        input_output_aliases={0: 0} if given else {},
        compiler_params=limits(),
        name="place_columns",
    )(*given, *arrays)


def body(sizes, parts, params, momentum, gradient, chosen_rows, live_counts, common_rows):
    matrix = dct_table(params.shape[0])
    forward, back = jnp.asarray(split_table(matrix)), jnp.asarray(split_table(matrix.T))
    chosen = jnp.transpose(chosen_rows[0, 0])
    counts = live_counts[0]
    common = jnp.transpose(common_rows[0])
    sent = pick(forward, momentum, gradient, chosen, counts, common, parts)
    piece = functools.partial(rest, back, sent, momentum, gradient, chosen, counts)
    if sizes is not None:
        got = lax.all_to_all(sent, EVERY, 0, 0, tiled=True)
        mine = add_up(back, got, params)
        new_params, residual = spread(mine, piece, params, sizes)
    else:
        residual = piece(0, parts, None)
        new_params = plain_update(back, sent, params)
    return new_params, residual


def plain_update(back, sent, params):
    order, columns = params.shape
    got = lax.all_to_all(sent, "col", 0, 0, tiled=True)
    got = lax.all_gather(got, "row", axis=0, tiled=True)
    width = columns // sent.shape[0]
    row = got[:, :, width : width + width // order].astype(jnp.int32)
    row = jnp.repeat(row, order, axis=2)
    table = row[:, :, None, :] == jnp.arange(order, dtype=jnp.int32)[:, None]
    total = jnp.sum(jnp.where(table, got[:, :, None, :width], 0.0), axis=(0, 1))
    total = lax.all_gather(total, "col", axis=1, tiled=True)
    return params - step_size * product(back, total)


def solution(mesh):
    rows, cols = mesh.shape["row"], mesh.shape["col"]
    placed = (
        P(),
        P("row", "col", None, None),
        P("row", "col", None, None),
        P("row", "col", None, None),
        P("row", "col", None),
        P("col", None, None),
    )

    def step(params, *rest_of):
        columns = params.shape[1]
        side = rows // CORES
        depth = cols // max(side, 1)
        whole = rows == side * CORES and cols == side * depth
        powers = all(n > 0 and n & (n - 1) == 0 for n in (side, depth))
        shared = columns % (rows * cols * LANES) == 0
        sizes = (side, depth, side) if whole and powers and shared else None
        parts = cols if sizes is None else rows * cols
        return jax.shard_map(
            functools.partial(body, sizes, parts),
            mesh=mesh,
            in_specs=placed,
            out_specs=(P(), P("row", "col", None, None)),
            check_vma=False,
        )(params, *rest_of)

    return step
```

```python
import functools
import math

import jax
import jax.numpy as jnp
import ml_dtypes
import numpy as np
from jax import lax
from jax.experimental import pallas as pl
from jax.experimental.pallas import tpu as pltpu
from jax.sharding import PartitionSpec as P

decay_rate = 0.9
step_size = 0.1
LANES = 128
SUB = 8
CORES = 2
MESSAGE_ROWS = 2
EVERY = ("row", "col")
VMEM_BYTES = 48 * 1024 * 1024


def dct_table(order):
    freq = np.arange(order, dtype=np.float64)[:, None]
    place = np.arange(order, dtype=np.float64)[None, :]
    matrix = math.sqrt(2.0 / order) * np.cos(math.pi * (2.0 * place + 1.0) * freq / (2.0 * order))
    return np.where(freq == 0.0, matrix * math.sqrt(0.5), matrix)


def split_table(matrix):
    high = matrix.astype(ml_dtypes.bfloat16)
    low = (matrix - high.astype(np.float64)).astype(ml_dtypes.bfloat16)
    return np.concatenate([high, low, high], axis=1)


def product(table, field):
    high = field.astype(jnp.bfloat16)
    low = (field - high.astype(jnp.float32)).astype(jnp.bfloat16)
    stacked = jnp.concatenate([high, high, low], axis=0)
    return jnp.dot(table, stacked, preferred_element_type=jnp.float32)


def pick_kernel(width, steps, slots_of, *refs):
    sources, out_ref, held, arrived = refs[:6], refs[6], refs[7:13], refs[13]
    table_ref, chosen_ref, counts_ref, common_ref, m_ref, g_ref = held
    order, columns = m_ref.shape
    step = columns // steps
    copies = [
        pltpu.make_async_copy(source, target, arrived.at[n])
        for n, (source, target) in enumerate(zip(sources[:4], held[:4], strict=True))
    ]
    for i in range(steps):
        cut = pl.ds(i * step, step)
        for source, target in zip(sources[4:], held[4:], strict=True):
            copies.append(
                pltpu.make_async_copy(
                    source.at[0, 0, :, cut], target.at[:, cut], arrived.at[len(copies)]
                )
            )
    for copy in copies:
        copy.start()
    for copy in copies[:4]:
        copy.wait()
    chosen = chosen_ref[...]
    common = common_ref[...]
    slots = chosen.shape[0]
    slot = lax.broadcasted_iota(jnp.int32, chosen.shape, 0)
    inside = chosen == common[0:1]
    for q in range(1, common.shape[0]):
        inside = inside | (chosen == common[q : q + 1])
    live = jnp.where(slot < counts_ref[...], chosen, -1)
    rows = jnp.where(inside, live, -1)
    live = jnp.concatenate([live, live], axis=0)
    rows = jnp.concatenate([rows, rows], axis=0)
    share = width // order
    for i in range(steps):
        for copy in copies[4 + 2 * i : 6 + 2 * i]:
            copy.wait()
        for part in range(i * step // width, (i + 1) * step // width):
            cut = pl.ds(part * width, width)
            spectrum = product(table_ref[...], decay_rate * m_ref[:, cut] + g_ref[:, cut])
            for t in range(width // LANES):
                row = block_lanes(live, order, (part * width + t * LANES) // order)
                tile, within = row >> 3, row & 7
                picked = jnp.zeros((SUB, LANES), jnp.float32)
                for r in range(order // SUB):
                    here = spectrum[r * SUB : (r + 1) * SUB, t * LANES : (t + 1) * LANES]
                    here = jnp.take_along_axis(here, within, axis=0)
                    picked = jnp.where(tile == r, here, picked)
                for s in range(0, slots, MESSAGE_ROWS):
                    for to in slots_of[part]:
                        out_ref[to, :, columns_of(width, s, t * LANES)] = picked[
                            s : s + MESSAGE_ROWS
                        ]
            lanes = lax.broadcasted_iota(jnp.int32, (SUB, LANES), 1)
            each = LANES * MESSAGE_ROWS // slots
            numbers = jnp.zeros((MESSAGE_ROWS, LANES), jnp.float32)
            for s in range(0, slots, MESSAGE_ROWS):
                from_s = lanes - s // MESSAGE_ROWS * each
                from_s = part * share + jnp.clip(from_s, 0, share - 1)
                from_s = take_blocks(rows, from_s, part * share)[s : s + MESSAGE_ROWS]
                mine = lanes[:MESSAGE_ROWS] // each == s // MESSAGE_ROWS
                numbers = jnp.where(mine, from_s.astype(jnp.float32), numbers)
            for to in slots_of[part]:
                out_ref[to, :, slots // MESSAGE_ROWS * width :] = numbers


def message_shape(slots, width):
    return MESSAGE_ROWS, slots // MESSAGE_ROWS * width + LANES


def columns_of(width, slot, at):
    first = slot // MESSAGE_ROWS * width + at
    return slice(first, first + LANES)


def take_blocks(rows, lanes, first):
    base = first // LANES * LANES
    return jnp.take_along_axis(rows[:, base : base + LANES], lanes - base, axis=1)


def block_lanes(rows, order, first):
    lanes = first + lax.broadcasted_iota(jnp.int32, (SUB, LANES), 1) // order
    return take_blocks(rows, lanes, first)


def rest_kernel(skipped, start, width, slot_of, *refs):
    back_ref, chosen_ref, counts_ref, sent_ref, m_ref, g_ref, out_ref, held, gone = refs[skipped:]
    order, columns = held.shape
    chosen = chosen_ref[...]
    slots = chosen.shape[0]
    slot = lax.broadcasted_iota(jnp.int32, chosen.shape, 0)
    live = jnp.where(slot < counts_ref[...], chosen, -1)
    live = jnp.concatenate([live, live], axis=0)
    sub = lax.broadcasted_iota(jnp.int32, (SUB, LANES), 0)
    copies = []
    for part in range(columns // width):
        parts = []
        for t in range(width // LANES):
            values = [
                sent_ref[
                    slot_of[start + part],
                    s % MESSAGE_ROWS : s % MESSAGE_ROWS + 1,
                    columns_of(width, s, t * LANES),
                ]
                for s in range(slots)
            ]
            rows = block_lanes(live, order, ((start + part) * width + t * LANES) // order)
            wide = [
                (
                    jnp.broadcast_to(rows[s : s + 1], (SUB, LANES)) - sub,
                    jnp.broadcast_to(values[s], (SUB, LANES)),
                )
                for s in range(slots)
            ]
            tiles = []
            for r in range(order // SUB):
                tile = jnp.zeros((SUB, LANES), jnp.float32)
                for row, value in wide:
                    tile = jnp.where(row == r * SUB, value, tile)
                tiles.append(tile)
            parts.append(jnp.concatenate(tiles, axis=0))
        back = product(back_ref[...], jnp.concatenate(parts, axis=1))
        cut, here = pl.ds((start + part) * width, width), pl.ds(part * width, width)
        held[:, here] = decay_rate * m_ref[0, 0, :, cut] + g_ref[0, 0, :, cut] - back
        copy = pltpu.make_async_copy(held.at[:, here], out_ref.at[0, 0, :, cut], gone.at[part])
        copy.start()
        copies.append(copy)
    for copy in copies:
        copy.wait()


def part_index(sizes, row, col, xor=(0, 0, 0), core_xor=0):
    y_size, z_size, x_size, lines = sizes
    y, core = row // CORES, (row % CORES) ^ core_xor
    z, x = (col // x_size) % lines, col % x_size
    return (((y ^ xor[0]) * CORES + core) * lines + (z ^ xor[1])) * x_size + (x ^ xor[2])


def sum_kernel(sizes, back_ref, got_ref, params_ref, out_ref, held, arrived):
    order, width = out_ref.shape
    me = part_index(sizes, lax.axis_index("row"), lax.axis_index("col"))
    copy = pltpu.make_async_copy(
        params_ref.at[:, pl.ds(pl.multiple_of(me * width, LANES), width)], held, arrived
    )
    copy.start()
    lists = got_ref.shape[0]
    chunks = (got_ref.shape[2] - LANES) // width
    each = LANES // chunks
    numbers = jnp.concatenate([got_ref[n, :, chunks * width :] for n in range(lists)], axis=0)
    numbers = jnp.transpose(numbers)
    freq = lax.broadcasted_iota(jnp.int32, (order, numbers.shape[1]), 0).astype(jnp.float32)
    lane = lax.broadcasted_iota(jnp.int32, (order, LANES), 1)
    pair = LANES // order
    totals = []
    for at in range(0, width, LANES):
        table = [
            jnp.concatenate(
                [
                    (numbers[c * each + block : c * each + block + 1] == freq).astype(jnp.float32)
                    for c in range(chunks)
                ],
                axis=1,
            )
            for block in range(at // order, at // order + pair)
        ]
        table = jnp.concatenate(table, axis=0).astype(jnp.bfloat16)
        values = jnp.concatenate(
            [
                got_ref[n, :, c * width + at : c * width + at + LANES]
                for c in range(chunks)
                for n in range(lists)
            ],
            axis=0,
        )
        high = values.astype(jnp.bfloat16)
        low = (values - high.astype(jnp.float32)).astype(jnp.bfloat16)
        total = jnp.dot(table, high, preferred_element_type=jnp.float32)
        total += jnp.dot(table, low, preferred_element_type=jnp.float32)
        mine = total[:order]
        for p in range(1, pair):
            mine = jnp.where(lane // order == p, total[p * order : (p + 1) * order], mine)
        totals.append(mine)
    update = product(back_ref[...], jnp.concatenate(totals, axis=1))
    copy.wait()
    out_ref[...] = held[...] - step_size * update


def place_kernel(places, sizes, skipped, *refs):
    *pieces, out_ref, sems = refs[skipped:]
    row, col = lax.axis_index("row"), lax.axis_index("col")
    copies = []
    for piece, (other, dy, dx, dz) in zip(pieces, places, strict=True):
        width = piece.shape[-1]
        part = part_index(sizes, row, col, (dy, dz, dx), other)
        copy = pltpu.make_async_copy(
            piece,
            out_ref.at[:, pl.ds(pl.multiple_of(part * width, LANES), width)],
            sems.at[len(copies)],
        )
        copy.start()
        copies.append(copy)
    for copy in copies:
        copy.wait()


def in_hbm(array):
    return pltpu.with_memory_space_constraint(array, pltpu.HBM)


def vmem():
    return pl.BlockSpec(memory_space=pltpu.VMEM)


def limits():
    return pltpu.CompilerParams(vmem_limit_bytes=VMEM_BYTES)


def list_spec(rows, step):
    return pl.BlockSpec((rows, LANES), lambda i: (0, i * step // LANES))


def pick(forward, momentum, gradient, chosen, counts, common, part_of):
    order, columns = momentum.shape[-2:]
    parts = max(part_of) + 1
    slots_of = [[to for to, part in enumerate(part_of) if part == p] for p in range(parts)]
    width = columns // parts
    steps = min(4, parts)
    slots = chosen.shape[0]
    sources = (forward, chosen, counts, common, momentum, gradient)
    held = [pltpu.VMEM(source.shape[-2:], source.dtype) for source in sources]
    return pl.pallas_call(
        functools.partial(pick_kernel, width, steps, slots_of),
        in_specs=[pl.BlockSpec(memory_space=pltpu.HBM)] * len(sources),
        out_specs=vmem(),
        out_shape=jax.ShapeDtypeStruct((len(part_of), *message_shape(slots, width)), jnp.float32),
        scratch_shapes=held + [pltpu.SemaphoreType.DMA((4 + 2 * steps,))],
        compiler_params=limits(),
        name="pick_rows",
    )(*map(in_hbm, sources))


def rest(slot_of, back, sent, momentum, gradient, chosen, counts, first, parts, before):
    order = momentum.shape[-2]
    width = momentum.shape[-1] // len(slot_of)
    anywhere = pl.BlockSpec(memory_space=pl.ANY)
    given = [] if before is None else [before]
    return pl.pallas_call(
        functools.partial(rest_kernel, len(given), first, width, slot_of),
        in_specs=[anywhere] * len(given) + [vmem()] * 6,
        out_specs=anywhere,
        out_shape=jax.ShapeDtypeStruct(momentum.shape, jnp.float32),
        scratch_shapes=[
            pltpu.VMEM((order, parts * width), jnp.float32),
            pltpu.SemaphoreType.DMA((parts,)),
        ],
        input_output_aliases={0: 0} if given else {},
        compiler_params=limits(),
        name="residual",
        cost_estimate=pl.CostEstimate(
            flops=12 * order * order * momentum.shape[-1] * (1 if before is None else 100),
            bytes_accessed=3 * momentum.size * 4 * (1 if before is None else 100),
            transcendentals=0,
        ),
    )(*given, back, chosen, counts, sent, momentum, gradient)


def add_up(sizes, parts, back, got, params):
    order = params.shape[0]
    width = params.shape[1] // parts
    return pl.pallas_call(
        functools.partial(sum_kernel, sizes),
        in_specs=[vmem(), vmem(), pl.BlockSpec(memory_space=pltpu.HBM)],
        out_specs=vmem(),
        out_shape=jax.ShapeDtypeStruct((order, width), jnp.float32),
        scratch_shapes=[pltpu.VMEM((order, width), jnp.float32), pltpu.SemaphoreType.DMA],
        compiler_params=limits(),
        name="sum_and_update",
    )(back, got, in_hbm(params))


def spread(mine, piece, params, sizes):
    y_size, z_size, x_size, lines = sizes

    def swap(array, by):
        pairs = []
        for y in range(y_size):
            for core in range(CORES):
                for z in range(z_size):
                    for x in range(x_size):
                        here = ((y * CORES + core) * z_size + z) * x_size + x
                        there = ((y ^ by[0]) * CORES + (core ^ by[1])) * z_size + (z ^ by[2])
                        pairs.append((here, there * x_size + (x ^ by[3])))
        return lax.ppermute(array, EVERY, pairs)

    far = [(j, i) for j in range(y_size) for i in range(x_size) if j or i]
    far.sort(key=lambda at: sum(map(bool, at)))
    parts = y_size * CORES * lines * x_size
    fill = parts * 15 // 16
    line = [mine] + [swap(mine, (0, 0, j, 0)) for j in range(1, lines)]
    early, late, done, residual = [], [], 0, None
    for n, own in enumerate(line):
        if n:
            residual = piece(done, fill, residual)
            own, residual = lax.optimization_barrier((own, residual))
            done += fill
        early.append((own, 0, 0, n))
        sent = [(swap(own, (j, 0, 0, i)), j, i, n) for j, i in far]
        if n == lines - 1:
            late += sent
        else:
            early += sent
    residual = piece(done, parts - done, residual)

    def other(piece_of):
        return (swap(piece_of[0], (0, 1, 0, 0)), 1, *piece_of[1:])

    near = [piece_of for piece_of in early if not (piece_of[1] or piece_of[2])]
    gone = [piece_of for piece_of in early if piece_of[1] or piece_of[2]]
    first = [(array, 0, *at) for array, *at in early] + [other(piece_of) for piece_of in near]
    partial = place(first, sizes, params, None)
    arrays = [piece_of[0] for piece_of in late]
    arrays, residual, partial = lax.optimization_barrier((arrays, residual, partial))
    late = [(array, *at[1:]) for array, at in zip(arrays, late, strict=True)]
    partial = place([(array, 0, *at) for array, *at in late], sizes, params, partial)
    partial = place([other(piece_of) for piece_of in gone + late], sizes, params, partial)
    return partial, residual


def place(pieces, sizes, params, partial):
    arrays = [piece[0] for piece in pieces]
    places = [piece[1:] for piece in pieces]
    anywhere = pl.BlockSpec(memory_space=pl.ANY)
    given = [] if partial is None else [partial]
    return pl.pallas_call(
        functools.partial(place_kernel, places, sizes, len(given)),
        in_specs=[anywhere] * (len(given) + len(arrays)),
        out_specs=anywhere,
        out_shape=jax.ShapeDtypeStruct(params.shape, jnp.float32),
        scratch_shapes=[pltpu.SemaphoreType.DMA((len(arrays),))],
        input_output_aliases={0: 0} if given else {},
        compiler_params=limits(),
        name="place_columns",
    )(*given, *arrays)


def body(sizes, part_of, params, momentum, gradient, chosen_rows, live_counts, common_rows):
    matrix = dct_table(params.shape[0])
    forward, back = jnp.asarray(split_table(matrix)), jnp.asarray(split_table(matrix.T))
    chosen = jnp.transpose(chosen_rows[0, 0])
    counts = live_counts[0]
    common = jnp.transpose(common_rows[0])
    sent = pick(forward, momentum, gradient, chosen, counts, common, part_of)
    parts = max(part_of) + 1
    slot_of = [part_of.index(part) for part in range(parts)]
    piece = functools.partial(rest, slot_of, back, sent, momentum, gradient, chosen, counts)
    if sizes is not None:
        got = lax.all_to_all(sent, EVERY, 0, 0, tiled=True)
        mine = add_up(sizes, parts, back, got, params)
        new_params, residual = spread(mine, piece, params, sizes)
    else:
        residual = piece(0, parts, None)
        new_params = plain_update(back, sent, params)
    return new_params, residual


def plain_update(back, sent, params):
    order, columns = params.shape
    got = lax.all_to_all(sent, "col", 0, 0, tiled=True)
    got = lax.all_gather(got, "row", axis=0, tiled=True)
    width = columns // sent.shape[0]
    chunks = (got.shape[2] - LANES) // width
    values = got[:, :, : chunks * width].reshape(*got.shape[:2], chunks, width)
    numbers = got[:, :, chunks * width :].reshape(*got.shape[:2], chunks, -1)
    row = jnp.repeat(numbers[..., : width // order].astype(jnp.int32), order, axis=3)
    table = row[..., None, :] == jnp.arange(order, dtype=jnp.int32)[:, None]
    total = jnp.sum(jnp.where(table, values[..., None, :], 0.0), axis=(0, 1, 2))
    total = lax.all_gather(total, "col", axis=1, tiled=True)
    return params - step_size * product(back, total)


def plan(rows, cols, columns):
    side = rows // CORES
    depth = cols // max(side, 1)
    whole = rows == side * CORES and cols == side * depth
    if not whole or any(n < 1 or n & (n - 1) for n in (side, depth)):
        return None
    lines = max(depth // 2, 1)
    while lines > 1 and columns % (side * CORES * lines * side * LANES):
        lines //= 2
    if columns % (side * CORES * lines * side * LANES):
        return None
    return side, depth, side, lines


def solution(mesh):
    rows, cols = mesh.shape["row"], mesh.shape["col"]
    placed = (
        P(),
        P("row", "col", None, None),
        P("row", "col", None, None),
        P("row", "col", None, None),
        P("row", "col", None),
        P("col", None, None),
    )

    def step(params, *rest_of):
        sizes = plan(rows, cols, params.shape[1])
        part_of = list(range(cols))
        if sizes is not None:
            part_of = [part_index(sizes, r, c) for r in range(rows) for c in range(cols)]
        return jax.shard_map(
            functools.partial(body, sizes, part_of),
            mesh=mesh,
            in_specs=placed,
            out_specs=(P(), P("row", "col", None, None)),
            check_vma=False,
        )(params, *rest_of)

    return step
```

```python
import functools
import math

import jax
import jax.numpy as jnp
import ml_dtypes
import numpy as np
from jax import lax
from jax.experimental import pallas as pl
from jax.experimental.pallas import tpu as pltpu
from jax.sharding import PartitionSpec as P

decay_rate = 0.9
step_size = 0.1
LANES = 128
SUB = 8
CORES = 2
MESSAGE_ROWS = 2
EVERY = ("row", "col")
VMEM_BYTES = 48 * 1024 * 1024


def dct_table(order):
    freq = np.arange(order, dtype=np.float64)[:, None]
    place = np.arange(order, dtype=np.float64)[None, :]
    matrix = math.sqrt(2.0 / order) * np.cos(math.pi * (2.0 * place + 1.0) * freq / (2.0 * order))
    return np.where(freq == 0.0, matrix * math.sqrt(0.5), matrix)


def split_table(matrix):
    high = matrix.astype(ml_dtypes.bfloat16)
    low = (matrix - high.astype(np.float64)).astype(ml_dtypes.bfloat16)
    return np.concatenate([high, low, high], axis=1)


def product(table, field):
    high = field.astype(jnp.bfloat16)
    low = (field - high.astype(jnp.float32)).astype(jnp.bfloat16)
    stacked = jnp.concatenate([high, high, low], axis=0)
    return jnp.dot(table, stacked, preferred_element_type=jnp.float32)


def pick_kernel(width, steps, slots_of, *refs):
    sources, out_ref, held, arrived = refs[:6], refs[6], refs[7:13], refs[13]
    table_ref, chosen_ref, counts_ref, common_ref, m_ref, g_ref = held
    order, columns = m_ref.shape
    step = columns // steps
    copies = [
        pltpu.make_async_copy(source, target, arrived.at[n])
        for n, (source, target) in enumerate(zip(sources[:4], held[:4], strict=True))
    ]
    for i in range(steps):
        cut = pl.ds(i * step, step)
        for source, target in zip(sources[4:], held[4:], strict=True):
            copies.append(
                pltpu.make_async_copy(
                    source.at[0, 0, :, cut], target.at[:, cut], arrived.at[len(copies)]
                )
            )
    for copy in copies:
        copy.start()
    for copy in copies[:4]:
        copy.wait()
    chosen = chosen_ref[...]
    common = common_ref[...]
    slots = chosen.shape[0]
    slot = lax.broadcasted_iota(jnp.int32, chosen.shape, 0)
    inside = chosen == common[0:1]
    for q in range(1, common.shape[0]):
        inside = inside | (chosen == common[q : q + 1])
    live = jnp.where(slot < counts_ref[...], chosen, -1)
    rows = jnp.where(inside, live, -1)
    live = jnp.concatenate([live, live], axis=0)
    rows = jnp.concatenate([rows, rows], axis=0)
    share = width // order
    for i in range(steps):
        for copy in copies[4 + 2 * i : 6 + 2 * i]:
            copy.wait()
        for part in range(i * step // width, (i + 1) * step // width):
            cut = pl.ds(part * width, width)
            spectrum = product(table_ref[...], decay_rate * m_ref[:, cut] + g_ref[:, cut])
            for t in range(width // LANES):
                row = block_lanes(live, order, (part * width + t * LANES) // order)
                tile, within = row >> 3, row & 7
                picked = jnp.zeros((SUB, LANES), jnp.float32)
                for r in range(order // SUB):
                    here = spectrum[r * SUB : (r + 1) * SUB, t * LANES : (t + 1) * LANES]
                    here = jnp.take_along_axis(here, within, axis=0)
                    picked = jnp.where(tile == r, here, picked)
                for s in range(0, slots, MESSAGE_ROWS):
                    for to in slots_of[part]:
                        out_ref[to, :, columns_of(width, s, t * LANES)] = picked[
                            s : s + MESSAGE_ROWS
                        ]
            lanes = lax.broadcasted_iota(jnp.int32, (SUB, LANES), 1)
            each = LANES * MESSAGE_ROWS // slots
            numbers = jnp.zeros((MESSAGE_ROWS, LANES), jnp.float32)
            for s in range(0, slots, MESSAGE_ROWS):
                from_s = lanes - s // MESSAGE_ROWS * each
                from_s = part * share + jnp.clip(from_s, 0, share - 1)
                from_s = take_blocks(rows, from_s, part * share)[s : s + MESSAGE_ROWS]
                mine = lanes[:MESSAGE_ROWS] // each == s // MESSAGE_ROWS
                numbers = jnp.where(mine, from_s.astype(jnp.float32), numbers)
            for to in slots_of[part]:
                out_ref[to, :, slots // MESSAGE_ROWS * width :] = numbers


def message_shape(slots, width):
    return MESSAGE_ROWS, slots // MESSAGE_ROWS * width + LANES


def columns_of(width, slot, at):
    first = slot // MESSAGE_ROWS * width + at
    return slice(first, first + LANES)


def take_blocks(rows, lanes, first):
    base = first // LANES * LANES
    return jnp.take_along_axis(rows[:, base : base + LANES], lanes - base, axis=1)


def block_lanes(rows, order, first):
    lanes = first + lax.broadcasted_iota(jnp.int32, (SUB, LANES), 1) // order
    return take_blocks(rows, lanes, first)


def rest_kernel(skipped, start, width, slot_of, *refs):
    back_ref, chosen_ref, counts_ref, sent_ref, m_ref, g_ref, out_ref, held, gone = refs[skipped:]
    order, columns = held.shape
    chosen = chosen_ref[...]
    slots = chosen.shape[0]
    slot = lax.broadcasted_iota(jnp.int32, chosen.shape, 0)
    live = jnp.where(slot < counts_ref[...], chosen, -1)
    live = jnp.concatenate([live, live], axis=0)
    sub = lax.broadcasted_iota(jnp.int32, (SUB, LANES), 0)
    copies = []
    for part in range(columns // width):
        parts = []
        for t in range(width // LANES):
            values = [
                sent_ref[
                    slot_of[start + part],
                    s % MESSAGE_ROWS : s % MESSAGE_ROWS + 1,
                    columns_of(width, s, t * LANES),
                ]
                for s in range(slots)
            ]
            rows = block_lanes(live, order, ((start + part) * width + t * LANES) // order)
            wide = [
                (
                    jnp.broadcast_to(rows[s : s + 1], (SUB, LANES)) - sub,
                    jnp.broadcast_to(values[s], (SUB, LANES)),
                )
                for s in range(slots)
            ]
            tiles = []
            for r in range(order // SUB):
                tile = jnp.zeros((SUB, LANES), jnp.float32)
                for row, value in wide:
                    tile = jnp.where(row == r * SUB, value, tile)
                tiles.append(tile)
            parts.append(jnp.concatenate(tiles, axis=0))
        back = product(back_ref[...], jnp.concatenate(parts, axis=1))
        cut, here = pl.ds((start + part) * width, width), pl.ds(part * width, width)
        held[:, here] = decay_rate * m_ref[0, 0, :, cut] + g_ref[0, 0, :, cut] - back
        copy = pltpu.make_async_copy(held.at[:, here], out_ref.at[0, 0, :, cut], gone.at[part])
        copy.start()
        copies.append(copy)
    for copy in copies:
        copy.wait()


def part_index(sizes, row, col, xor=(0, 0, 0), core_xor=0):
    y_size, z_size, x_size, lines = sizes
    y, core = row // CORES, (row % CORES) ^ core_xor
    z, x = (col // x_size) % lines, col % x_size
    return (((y ^ xor[0]) * CORES + core) * lines + (z ^ xor[1])) * x_size + (x ^ xor[2])


def sum_kernel(sizes, back_ref, got_ref, params_ref, out_ref, held, arrived):
    order, width = out_ref.shape
    me = part_index(sizes, lax.axis_index("row"), lax.axis_index("col"))
    copy = pltpu.make_async_copy(
        params_ref.at[:, pl.ds(pl.multiple_of(me * width, LANES), width)], held, arrived
    )
    copy.start()
    lists = got_ref.shape[0]
    chunks = (got_ref.shape[2] - LANES) // width
    each = LANES // chunks
    numbers = jnp.concatenate([got_ref[n, :, chunks * width :] for n in range(lists)], axis=0)
    numbers = jnp.transpose(numbers)
    freq = lax.broadcasted_iota(jnp.int32, (order, numbers.shape[1]), 0).astype(jnp.float32)
    lane = lax.broadcasted_iota(jnp.int32, (order, LANES), 1)
    pair = LANES // order
    totals = []
    for at in range(0, width, LANES):
        table = [
            jnp.concatenate(
                [
                    (numbers[c * each + block : c * each + block + 1] == freq).astype(jnp.float32)
                    for c in range(chunks)
                ],
                axis=1,
            )
            for block in range(at // order, at // order + pair)
        ]
        table = jnp.concatenate(table, axis=0).astype(jnp.bfloat16)
        values = jnp.concatenate(
            [
                got_ref[n, :, c * width + at : c * width + at + LANES]
                for c in range(chunks)
                for n in range(lists)
            ],
            axis=0,
        )
        high = values.astype(jnp.bfloat16)
        low = (values - high.astype(jnp.float32)).astype(jnp.bfloat16)
        total = jnp.dot(table, high, preferred_element_type=jnp.float32)
        total += jnp.dot(table, low, preferred_element_type=jnp.float32)
        mine = total[:order]
        for p in range(1, pair):
            mine = jnp.where(lane // order == p, total[p * order : (p + 1) * order], mine)
        totals.append(mine)
    update = product(back_ref[...], jnp.concatenate(totals, axis=1))
    copy.wait()
    out_ref[...] = held[...] - step_size * update


def place_kernel(places, sizes, skipped, *refs):
    *pieces, out_ref, sems = refs[skipped:]
    row, col = lax.axis_index("row"), lax.axis_index("col")
    copies = []
    for piece, (other, dy, dx, dz) in zip(pieces, places, strict=True):
        width = piece.shape[-1]
        part = part_index(sizes, row, col, (dy, dz, dx), other)
        copy = pltpu.make_async_copy(
            piece,
            out_ref.at[:, pl.ds(pl.multiple_of(part * width, LANES), width)],
            sems.at[len(copies)],
        )
        copy.start()
        copies.append(copy)
    for copy in copies:
        copy.wait()


def in_hbm(array):
    return pltpu.with_memory_space_constraint(array, pltpu.HBM)


def vmem():
    return pl.BlockSpec(memory_space=pltpu.VMEM)


def limits():
    return pltpu.CompilerParams(vmem_limit_bytes=VMEM_BYTES)


def list_spec(rows, step):
    return pl.BlockSpec((rows, LANES), lambda i: (0, i * step // LANES))


def pick(forward, momentum, gradient, chosen, counts, common, part_of):
    order, columns = momentum.shape[-2:]
    parts = max(part_of) + 1
    slots_of = [[to for to, part in enumerate(part_of) if part == p] for p in range(parts)]
    width = columns // parts
    steps = min(4, parts)
    slots = chosen.shape[0]
    sources = (forward, chosen, counts, common, momentum, gradient)
    held = [pltpu.VMEM(source.shape[-2:], source.dtype) for source in sources]
    return pl.pallas_call(
        functools.partial(pick_kernel, width, steps, slots_of),
        in_specs=[pl.BlockSpec(memory_space=pltpu.HBM)] * len(sources),
        out_specs=vmem(),
        out_shape=jax.ShapeDtypeStruct((len(part_of), *message_shape(slots, width)), jnp.float32),
        scratch_shapes=held + [pltpu.SemaphoreType.DMA((4 + 2 * steps,))],
        compiler_params=limits(),
        name="pick_rows",
    )(*map(in_hbm, sources))


def rest(slot_of, back, sent, momentum, gradient, chosen, counts, first, parts, before):
    order = momentum.shape[-2]
    width = momentum.shape[-1] // len(slot_of)
    anywhere = pl.BlockSpec(memory_space=pl.ANY)
    given = [] if before is None else [before]
    return pl.pallas_call(
        functools.partial(rest_kernel, len(given), first, width, slot_of),
        in_specs=[anywhere] * len(given) + [vmem()] * 6,
        out_specs=anywhere,
        out_shape=jax.ShapeDtypeStruct(momentum.shape, jnp.float32),
        scratch_shapes=[
            pltpu.VMEM((order, parts * width), jnp.float32),
            pltpu.SemaphoreType.DMA((parts,)),
        ],
        input_output_aliases={0: 0} if given else {},
        compiler_params=limits(),
        name="residual",
        cost_estimate=pl.CostEstimate(
            flops=12 * order * order * momentum.shape[-1] * (1 if before is None else 100),
            bytes_accessed=3 * momentum.size * 4 * (1 if before is None else 100),
            transcendentals=0,
        ),
    )(*given, back, chosen, counts, sent, momentum, gradient)


def add_up(sizes, parts, back, got, params):
    order = params.shape[0]
    width = params.shape[1] // parts
    return pl.pallas_call(
        functools.partial(sum_kernel, sizes),
        in_specs=[vmem(), vmem(), pl.BlockSpec(memory_space=pltpu.HBM)],
        out_specs=vmem(),
        out_shape=jax.ShapeDtypeStruct((order, width), jnp.float32),
        scratch_shapes=[pltpu.VMEM((order, width), jnp.float32), pltpu.SemaphoreType.DMA],
        compiler_params=limits(),
        name="sum_and_update",
    )(back, got, in_hbm(params))


def spread(mine, piece, params, sizes):
    y_size, z_size, x_size, lines = sizes

    def swap(array, by):
        pairs = []
        for y in range(y_size):
            for core in range(CORES):
                for z in range(z_size):
                    for x in range(x_size):
                        here = ((y * CORES + core) * z_size + z) * x_size + x
                        there = ((y ^ by[0]) * CORES + (core ^ by[1])) * z_size + (z ^ by[2])
                        pairs.append((here, there * x_size + (x ^ by[3])))
        return lax.ppermute(array, EVERY, pairs)

    far = [(j, i) for j in range(y_size) for i in range(x_size) if j or i]
    far.sort(key=lambda at: sum(map(bool, at)))
    parts = y_size * CORES * lines * x_size
    fill = parts * 12 // 16
    line = [mine] + [swap(mine, (0, 0, j, 0)) for j in range(1, lines)]
    def other(piece_of):
        return (swap(piece_of[0], (0, 1, 0, 0)), 1, *piece_of[1:])

    corners = [(j, i) for j, i in far if j and i]
    sides = [(j, i) for j, i in far if not (j and i)]
    near = [(own, 0, 0, n) for n, own in enumerate(line)]
    begun = [(swap(mine, (j, 0, 0, i)), j, i, 0) for j, i in corners]
    theirs = [other(near[0])]
    held, theirs_first = lax.optimization_barrier((mine, theirs[0][0]))
    theirs = [(theirs_first, *theirs[0][1:])]
    gone = begun + [(swap(held, (j, 0, 0, i)), j, i, 0) for j, i in sides]
    late, done, residual = [], 0, None
    for n, own in enumerate(line[1:], 1):
        residual = piece(done, fill, residual)
        own, residual = lax.optimization_barrier((own, residual))
        done += fill
        near[n] = (own, 0, 0, n)
        late += [(swap(own, (j, 0, 0, i)), j, i, n) for j, i in sides]
        late += [(swap(array, (0, 0, n, 0)), j, i, n) for array, j, i, _ in begun]
    residual = piece(done, parts - done, residual)
    waiting = near[1:] + gone
    arrays, residual = lax.optimization_barrier(([piece_of[0] for piece_of in waiting], residual))
    waiting = [(array, *at[1:]) for array, at in zip(arrays, waiting, strict=True)]
    first = [(array, 0, *at) for array, *at in near[:1] + waiting] + theirs
    partial = place(first, sizes, params, None)
    theirs = [other(piece_of) for piece_of in waiting]
    arrays = [piece_of[0] for piece_of in late]
    arrays, partial = lax.optimization_barrier((arrays, partial))
    late = [(array, *at[1:]) for array, at in zip(arrays, late, strict=True)]
    second = [(array, 0, *at) for array, *at in late] + theirs
    partial = place(second, sizes, params, partial)
    partial = place([other(piece_of) for piece_of in late], sizes, params, partial)
    return partial, residual


def place(pieces, sizes, params, partial):
    arrays = [piece[0] for piece in pieces]
    places = [piece[1:] for piece in pieces]
    anywhere = pl.BlockSpec(memory_space=pl.ANY)
    given = [] if partial is None else [partial]
    return pl.pallas_call(
        functools.partial(place_kernel, places, sizes, len(given)),
        in_specs=[anywhere] * (len(given) + len(arrays)),
        out_specs=anywhere,
        out_shape=jax.ShapeDtypeStruct(params.shape, jnp.float32),
        scratch_shapes=[pltpu.SemaphoreType.DMA((len(arrays),))],
        input_output_aliases={0: 0} if given else {},
        compiler_params=limits(),
        name="place_columns",
    )(*given, *arrays)


def body(sizes, part_of, params, momentum, gradient, chosen_rows, live_counts, common_rows):
    matrix = dct_table(params.shape[0])
    forward, back = jnp.asarray(split_table(matrix)), jnp.asarray(split_table(matrix.T))
    chosen = jnp.transpose(chosen_rows[0, 0])
    counts = live_counts[0]
    common = jnp.transpose(common_rows[0])
    sent = pick(forward, momentum, gradient, chosen, counts, common, part_of)
    parts = max(part_of) + 1
    slot_of = [part_of.index(part) for part in range(parts)]
    piece = functools.partial(rest, slot_of, back, sent, momentum, gradient, chosen, counts)
    if sizes is not None:
        got = lax.all_to_all(sent, EVERY, 0, 0, tiled=True)
        mine = add_up(sizes, parts, back, got, params)
        new_params, residual = spread(mine, piece, params, sizes)
    else:
        residual = piece(0, parts, None)
        new_params = plain_update(back, sent, params)
    return new_params, residual


def plain_update(back, sent, params):
    order, columns = params.shape
    got = lax.all_to_all(sent, "col", 0, 0, tiled=True)
    got = lax.all_gather(got, "row", axis=0, tiled=True)
    width = columns // sent.shape[0]
    chunks = (got.shape[2] - LANES) // width
    values = got[:, :, : chunks * width].reshape(*got.shape[:2], chunks, width)
    numbers = got[:, :, chunks * width :].reshape(*got.shape[:2], chunks, -1)
    row = jnp.repeat(numbers[..., : width // order].astype(jnp.int32), order, axis=3)
    table = row[..., None, :] == jnp.arange(order, dtype=jnp.int32)[:, None]
    total = jnp.sum(jnp.where(table, values[..., None, :], 0.0), axis=(0, 1, 2))
    total = lax.all_gather(total, "col", axis=1, tiled=True)
    return params - step_size * product(back, total)


def plan(rows, cols, columns):
    side = rows // CORES
    depth = cols // max(side, 1)
    whole = rows == side * CORES and cols == side * depth
    if not whole or any(n < 1 or n & (n - 1) for n in (side, depth)):
        return None
    lines = max(depth // 2, 1)
    while lines > 1 and columns % (side * CORES * lines * side * LANES):
        lines //= 2
    if columns % (side * CORES * lines * side * LANES):
        return None
    return side, depth, side, lines


def solution(mesh):
    rows, cols = mesh.shape["row"], mesh.shape["col"]
    placed = (
        P(),
        P("row", "col", None, None),
        P("row", "col", None, None),
        P("row", "col", None, None),
        P("row", "col", None),
        P("col", None, None),
    )

    def step(params, *rest_of):
        sizes = plan(rows, cols, params.shape[1])
        part_of = list(range(cols))
        if sizes is not None:
            part_of = [part_index(sizes, r, c) for r in range(rows) for c in range(cols)]
        return jax.shard_map(
            functools.partial(body, sizes, part_of),
            mesh=mesh,
            in_specs=placed,
            out_specs=(P(), P("row", "col", None, None)),
            check_vma=False,
        )(params, *rest_of)

    return step
```

```python
import functools
import math

import jax
import jax.numpy as jnp
import ml_dtypes
import numpy as np
from jax import lax
from jax.experimental import pallas as pl
from jax.experimental.pallas import tpu as pltpu
from jax.sharding import PartitionSpec as P

decay_rate = 0.9
step_size = 0.1
LANES = 128
SUB = 8
CORES = 2
MESSAGE_ROWS = 2
EVERY = ("row", "col")
VMEM_BYTES = 48 * 1024 * 1024


def dct_table(order):
    freq = np.arange(order, dtype=np.float64)[:, None]
    place = np.arange(order, dtype=np.float64)[None, :]
    matrix = math.sqrt(2.0 / order) * np.cos(math.pi * (2.0 * place + 1.0) * freq / (2.0 * order))
    return np.where(freq == 0.0, matrix * math.sqrt(0.5), matrix)


def split_table(matrix):
    high = matrix.astype(ml_dtypes.bfloat16)
    low = (matrix - high.astype(np.float64)).astype(ml_dtypes.bfloat16)
    return np.concatenate([high, low, high], axis=1)


def product(table, field):
    high = field.astype(jnp.bfloat16)
    low = (field - high.astype(jnp.float32)).astype(jnp.bfloat16)
    stacked = jnp.concatenate([high, high, low], axis=0)
    return jnp.dot(table, stacked, preferred_element_type=jnp.float32)


def pick_kernel(width, steps, slots_of, *refs):
    sources, out_ref, held, arrived = refs[:6], refs[6], refs[7:13], refs[13]
    table_ref, chosen_ref, counts_ref, common_ref, m_ref, g_ref = held
    order, columns = m_ref.shape
    step = columns // steps
    copies = [
        pltpu.make_async_copy(source, target, arrived.at[n])
        for n, (source, target) in enumerate(zip(sources[:4], held[:4], strict=True))
    ]
    for i in range(steps):
        cut = pl.ds(i * step, step)
        for source, target in zip(sources[4:], held[4:], strict=True):
            copies.append(
                pltpu.make_async_copy(
                    source.at[0, 0, :, cut], target.at[:, cut], arrived.at[len(copies)]
                )
            )
    for copy in copies:
        copy.start()
    for copy in copies[:4]:
        copy.wait()
    chosen = chosen_ref[...]
    common = common_ref[...]
    slots = chosen.shape[0]
    slot = lax.broadcasted_iota(jnp.int32, chosen.shape, 0)
    inside = chosen == common[0:1]
    for q in range(1, common.shape[0]):
        inside = inside | (chosen == common[q : q + 1])
    live = jnp.where(slot < counts_ref[...], chosen, -1)
    rows = jnp.where(inside, live, -1)
    live = jnp.concatenate([live, live], axis=0)
    rows = jnp.concatenate([rows, rows], axis=0)
    share = width // order
    for i in range(steps):
        for copy in copies[4 + 2 * i : 6 + 2 * i]:
            copy.wait()
        for part in range(i * step // width, (i + 1) * step // width):
            cut = pl.ds(part * width, width)
            spectrum = product(table_ref[...], decay_rate * m_ref[:, cut] + g_ref[:, cut])
            for t in range(width // LANES):
                row = block_lanes(live, order, (part * width + t * LANES) // order)
                tile, within = row >> 3, row & 7
                picked = jnp.zeros((SUB, LANES), jnp.float32)
                for r in range(order // SUB):
                    here = spectrum[r * SUB : (r + 1) * SUB, t * LANES : (t + 1) * LANES]
                    here = jnp.take_along_axis(here, within, axis=0)
                    picked = jnp.where(tile == r, here, picked)
                for s in range(0, slots, MESSAGE_ROWS):
                    for to in slots_of[part]:
                        out_ref[to, :, columns_of(width, s, t * LANES)] = picked[
                            s : s + MESSAGE_ROWS
                        ]
            lanes = lax.broadcasted_iota(jnp.int32, (SUB, LANES), 1)
            each = LANES * MESSAGE_ROWS // slots
            numbers = jnp.zeros((MESSAGE_ROWS, LANES), jnp.float32)
            for s in range(0, slots, MESSAGE_ROWS):
                from_s = lanes - s // MESSAGE_ROWS * each
                from_s = part * share + jnp.clip(from_s, 0, share - 1)
                from_s = take_blocks(rows, from_s, part * share)[s : s + MESSAGE_ROWS]
                mine = lanes[:MESSAGE_ROWS] // each == s // MESSAGE_ROWS
                numbers = jnp.where(mine, from_s.astype(jnp.float32), numbers)
            for to in slots_of[part]:
                out_ref[to, :, slots // MESSAGE_ROWS * width :] = numbers


def message_shape(slots, width):
    return MESSAGE_ROWS, slots // MESSAGE_ROWS * width + LANES


def columns_of(width, slot, at):
    first = slot // MESSAGE_ROWS * width + at
    return slice(first, first + LANES)


def take_blocks(rows, lanes, first):
    base = first // LANES * LANES
    return jnp.take_along_axis(rows[:, base : base + LANES], lanes - base, axis=1)


def block_lanes(rows, order, first):
    lanes = first + lax.broadcasted_iota(jnp.int32, (SUB, LANES), 1) // order
    return take_blocks(rows, lanes, first)


def rest_kernel(skipped, start, width, slot_of, *refs):
    back_ref, chosen_ref, counts_ref, sent_ref, m_ref, g_ref, out_ref, held, gone = refs[skipped:]
    order, columns = held.shape
    chosen = chosen_ref[...]
    slots = chosen.shape[0]
    slot = lax.broadcasted_iota(jnp.int32, chosen.shape, 0)
    live = jnp.where(slot < counts_ref[...], chosen, -1)
    live = jnp.concatenate([live, live], axis=0)
    sub = lax.broadcasted_iota(jnp.int32, (SUB, LANES), 0)
    copies = []
    for part in range(columns // width):
        parts = []
        for t in range(width // LANES):
            values = [
                sent_ref[
                    slot_of[start + part],
                    s % MESSAGE_ROWS : s % MESSAGE_ROWS + 1,
                    columns_of(width, s, t * LANES),
                ]
                for s in range(slots)
            ]
            rows = block_lanes(live, order, ((start + part) * width + t * LANES) // order)
            wide = [
                (
                    jnp.broadcast_to(rows[s : s + 1], (SUB, LANES)) - sub,
                    jnp.broadcast_to(values[s], (SUB, LANES)),
                )
                for s in range(slots)
            ]
            tiles = []
            for r in range(order // SUB):
                tile = jnp.zeros((SUB, LANES), jnp.float32)
                for row, value in wide:
                    tile = jnp.where(row == r * SUB, value, tile)
                tiles.append(tile)
            parts.append(jnp.concatenate(tiles, axis=0))
        back = product(back_ref[...], jnp.concatenate(parts, axis=1))
        cut, here = pl.ds((start + part) * width, width), pl.ds(part * width, width)
        held[:, here] = decay_rate * m_ref[0, 0, :, cut] + g_ref[0, 0, :, cut] - back
        copy = pltpu.make_async_copy(held.at[:, here], out_ref.at[0, 0, :, cut], gone.at[part])
        copy.start()
        copies.append(copy)
    for copy in copies:
        copy.wait()


def part_index(sizes, row, col, xor=(0, 0, 0), core_xor=0):
    y_size, z_size, x_size, lines = sizes
    y, core = row // CORES, (row % CORES) ^ core_xor
    z, x = (col // x_size) % lines, col % x_size
    return (((y ^ xor[0]) * CORES + core) * lines + (z ^ xor[1])) * x_size + (x ^ xor[2])


def sum_kernel(sizes, back_ref, got_ref, params_ref, out_ref, held, arrived):
    order, width = out_ref.shape
    me = part_index(sizes, lax.axis_index("row"), lax.axis_index("col"))
    copy = pltpu.make_async_copy(
        params_ref.at[:, pl.ds(pl.multiple_of(me * width, LANES), width)], held, arrived
    )
    copy.start()
    lists = got_ref.shape[0]
    chunks = (got_ref.shape[2] - LANES) // width
    each = LANES // chunks
    numbers = jnp.concatenate([got_ref[n, :, chunks * width :] for n in range(lists)], axis=0)
    numbers = jnp.transpose(numbers)
    freq = lax.broadcasted_iota(jnp.int32, (order, numbers.shape[1]), 0).astype(jnp.float32)
    lane = lax.broadcasted_iota(jnp.int32, (order, LANES), 1)
    pair = LANES // order
    totals = []
    for at in range(0, width, LANES):
        table = [
            jnp.concatenate(
                [
                    (numbers[c * each + block : c * each + block + 1] == freq).astype(jnp.float32)
                    for c in range(chunks)
                ],
                axis=1,
            )
            for block in range(at // order, at // order + pair)
        ]
        table = jnp.concatenate(table, axis=0).astype(jnp.bfloat16)
        values = jnp.concatenate(
            [
                got_ref[n, :, c * width + at : c * width + at + LANES]
                for c in range(chunks)
                for n in range(lists)
            ],
            axis=0,
        )
        high = values.astype(jnp.bfloat16)
        low = (values - high.astype(jnp.float32)).astype(jnp.bfloat16)
        total = jnp.dot(
            jnp.concatenate([table, table], axis=1),
            jnp.concatenate([high, low], axis=0),
            preferred_element_type=jnp.float32,
        )
        mine = total[:order]
        for p in range(1, pair):
            mine = jnp.where(lane // order == p, total[p * order : (p + 1) * order], mine)
        totals.append(mine)
    update = product(back_ref[...], jnp.concatenate(totals, axis=1))
    copy.wait()
    out_ref[...] = held[...] - step_size * update


def place_kernel(places, sizes, skipped, *refs):
    *pieces, out_ref, sems = refs[skipped:]
    row, col = lax.axis_index("row"), lax.axis_index("col")
    copies = []
    flat = [
        (piece.at[k] if len(piece.shape) == 3 else piece, place)
        for piece, among in zip(pieces, places, strict=True)
        for k, place in enumerate(among)
    ]
    for piece, (other, dy, dx, dz) in flat:
        width = piece.shape[-1]
        part = part_index(sizes, row, col, (dy, dz, dx), other)
        copy = pltpu.make_async_copy(
            piece,
            out_ref.at[:, pl.ds(pl.multiple_of(part * width, LANES), width)],
            sems.at[len(copies)],
        )
        copy.start()
        copies.append(copy)
    for copy in copies:
        copy.wait()


def in_hbm(array):
    return pltpu.with_memory_space_constraint(array, pltpu.HBM)


def vmem():
    return pl.BlockSpec(memory_space=pltpu.VMEM)


def limits():
    return pltpu.CompilerParams(vmem_limit_bytes=VMEM_BYTES)


def list_spec(rows, step):
    return pl.BlockSpec((rows, LANES), lambda i: (0, i * step // LANES))


def pick(forward, momentum, gradient, chosen, counts, common, part_of):
    order, columns = momentum.shape[-2:]
    parts = max(part_of) + 1
    slots_of = [[to for to, part in enumerate(part_of) if part == p] for p in range(parts)]
    width = columns // parts
    steps = min(4, parts)
    slots = chosen.shape[0]
    sources = (forward, chosen, counts, common, momentum, gradient)
    held = [pltpu.VMEM(source.shape[-2:], source.dtype) for source in sources]
    return pl.pallas_call(
        functools.partial(pick_kernel, width, steps, slots_of),
        in_specs=[pl.BlockSpec(memory_space=pltpu.HBM)] * len(sources),
        out_specs=vmem(),
        out_shape=jax.ShapeDtypeStruct((len(part_of), *message_shape(slots, width)), jnp.float32),
        scratch_shapes=held + [pltpu.SemaphoreType.DMA((4 + 2 * steps,))],
        compiler_params=limits(),
        name="pick_rows",
    )(*map(in_hbm, sources))


def rest(slot_of, back, sent, momentum, gradient, chosen, counts, first, parts, before):
    order = momentum.shape[-2]
    width = momentum.shape[-1] // len(slot_of)
    anywhere = pl.BlockSpec(memory_space=pl.ANY)
    given = [] if before is None else [before]
    return pl.pallas_call(
        functools.partial(rest_kernel, len(given), first, width, slot_of),
        in_specs=[anywhere] * len(given) + [vmem()] * 6,
        out_specs=anywhere,
        out_shape=jax.ShapeDtypeStruct(momentum.shape, jnp.float32),
        scratch_shapes=[
            pltpu.VMEM((order, parts * width), jnp.float32),
            pltpu.SemaphoreType.DMA((parts,)),
        ],
        input_output_aliases={0: 0} if given else {},
        compiler_params=limits(),
        name="residual",
        cost_estimate=pl.CostEstimate(
            flops=12 * order * order * momentum.shape[-1] * (1 if before is None else 1),
            bytes_accessed=3 * momentum.size * 4 * (1 if before is None else 1),
            transcendentals=0,
        ),
    )(*given, back, chosen, counts, sent, momentum, gradient)


def add_up(sizes, parts, back, got, params):
    order = params.shape[0]
    width = params.shape[1] // parts
    return pl.pallas_call(
        functools.partial(sum_kernel, sizes),
        in_specs=[vmem(), vmem(), pl.BlockSpec(memory_space=pltpu.HBM)],
        out_specs=vmem(),
        out_shape=jax.ShapeDtypeStruct((order, width), jnp.float32),
        scratch_shapes=[pltpu.VMEM((order, width), jnp.float32), pltpu.SemaphoreType.DMA],
        compiler_params=limits(),
        name="sum_and_update",
    )(back, got, in_hbm(params))


def spread(mine, piece, params, sizes):
    y_size, z_size, x_size, lines = sizes

    def swap(array, by):
        pairs = []
        for y in range(y_size):
            for core in range(CORES):
                for z in range(z_size):
                    for x in range(x_size):
                        here = ((y * CORES + core) * z_size + z) * x_size + x
                        there = ((y ^ by[0]) * CORES + (core ^ by[1])) * z_size + (z ^ by[2])
                        pairs.append((here, there * x_size + (x ^ by[3])))
        return lax.ppermute(array, EVERY, pairs)

    far = [(j, i) for j in range(y_size) for i in range(x_size) if j or i]
    far.sort(key=lambda at: sum(map(bool, at)))
    parts = y_size * CORES * lines * x_size
    fill = parts * 8 // 16
    line = [mine] + [swap(mine, (0, 0, j, 0)) for j in range(1, lines)]
    def mine_of(pieces):
        return [(array, [(0, *at)]) for array, *at in pieces]

    def other(pieces):
        arrays = [piece_of[0] for piece_of in pieces]
        array = arrays[0] if len(arrays) == 1 else jnp.stack(arrays)
        return (swap(array, (0, 1, 0, 0)), [(1, *piece_of[1:]) for piece_of in pieces])

    corners = [(j, i) for j, i in far if j and i]
    sides = [(j, i) for j, i in far if not (j and i)]
    near = [(own, 0, 0, n) for n, own in enumerate(line)]
    begun = [(swap(mine, (j, 0, 0, i)), j, i, 0) for j, i in corners]
    theirs = [other(near[:1])]
    held, theirs_first = lax.optimization_barrier((mine, theirs[0][0]))
    theirs = [(theirs_first, theirs[0][1])]
    gone = begun + [(swap(held, (j, 0, 0, i)), j, i, 0) for j, i in sides]
    late, done, residual = [], 0, None
    for n, own in enumerate(line[1:], 1):
        residual = piece(done, fill, residual)
        own, residual = lax.optimization_barrier((own, residual))
        done += fill
        near[n] = (own, 0, 0, n)
        late += [(swap(own, (j, 0, 0, i)), j, i, n) for j, i in sides]
        late += [(swap(array, (0, 0, n, 0)), j, i, n) for array, j, i, _ in begun]
    residual = piece(done, parts - done, residual)
    waiting = near[1:] + gone
    arrays, residual = lax.optimization_barrier(([piece_of[0] for piece_of in waiting], residual))
    waiting = [(array, *at[1:]) for array, at in zip(arrays, waiting, strict=True)]
    partial = place(mine_of(near[:1] + waiting) + theirs, sizes, params, None)
    theirs = [other(waiting[: -len(sides)]), other(waiting[-len(sides) :])]
    arrays = [piece_of[0] for piece_of in late]
    arrays, partial = lax.optimization_barrier((arrays, partial))
    late = [(array, *at[1:]) for array, at in zip(arrays, late, strict=True)]
    partial = place(mine_of(late) + theirs, sizes, params, partial)
    straight = [piece_of for piece_of in late if not (piece_of[1] and piece_of[2])]
    across = [piece_of for piece_of in late if piece_of[1] and piece_of[2]]
    partial = place([other(group) for group in (straight, across) if group], sizes, params, partial)
    return partial, residual


def place(pieces, sizes, params, partial):
    arrays = [piece[0] for piece in pieces]
    places = [piece[1] for piece in pieces]
    anywhere = pl.BlockSpec(memory_space=pl.ANY)
    given = [] if partial is None else [partial]
    return pl.pallas_call(
        functools.partial(place_kernel, places, sizes, len(given)),
        in_specs=[anywhere] * (len(given) + len(arrays)),
        out_specs=anywhere,
        out_shape=jax.ShapeDtypeStruct(params.shape, jnp.float32),
        scratch_shapes=[pltpu.SemaphoreType.DMA((sum(map(len, places)),))],
        input_output_aliases={0: 0} if given else {},
        compiler_params=limits(),
        name="place_columns",
    )(*given, *arrays)


def body(sizes, part_of, params, momentum, gradient, chosen_rows, live_counts, common_rows):
    matrix = dct_table(params.shape[0])
    forward, back = jnp.asarray(split_table(matrix)), jnp.asarray(split_table(matrix.T))
    chosen = jnp.transpose(chosen_rows[0, 0])
    counts = live_counts[0]
    common = jnp.transpose(common_rows[0])
    sent = pick(forward, momentum, gradient, chosen, counts, common, part_of)
    parts = max(part_of) + 1
    slot_of = [part_of.index(part) for part in range(parts)]
    piece = functools.partial(rest, slot_of, back, sent, momentum, gradient, chosen, counts)
    if sizes is not None:
        got = lax.all_to_all(sent, EVERY, 0, 0, tiled=True)
        mine = add_up(sizes, parts, back, got, params)
        new_params, residual = spread(mine, piece, params, sizes)
    else:
        residual = piece(0, parts, None)
        new_params = plain_update(back, sent, params)
    return new_params, residual


def plain_update(back, sent, params):
    order, columns = params.shape
    got = lax.all_to_all(sent, "col", 0, 0, tiled=True)
    got = lax.all_gather(got, "row", axis=0, tiled=True)
    width = columns // sent.shape[0]
    chunks = (got.shape[2] - LANES) // width
    values = got[:, :, : chunks * width].reshape(*got.shape[:2], chunks, width)
    numbers = got[:, :, chunks * width :].reshape(*got.shape[:2], chunks, -1)
    row = jnp.repeat(numbers[..., : width // order].astype(jnp.int32), order, axis=3)
    table = row[..., None, :] == jnp.arange(order, dtype=jnp.int32)[:, None]
    total = jnp.sum(jnp.where(table, values[..., None, :], 0.0), axis=(0, 1, 2))
    total = lax.all_gather(total, "col", axis=1, tiled=True)
    return params - step_size * product(back, total)


def plan(rows, cols, columns):
    side = rows // CORES
    depth = cols // max(side, 1)
    whole = rows == side * CORES and cols == side * depth
    if not whole or any(n < 1 or n & (n - 1) for n in (side, depth)):
        return None
    lines = max(depth // 2, 1)
    while lines > 1 and columns % (side * CORES * lines * side * LANES):
        lines //= 2
    if columns % (side * CORES * lines * side * LANES):
        return None
    return side, depth, side, lines


def solution(mesh):
    rows, cols = mesh.shape["row"], mesh.shape["col"]
    placed = (
        P(),
        P("row", "col", None, None),
        P("row", "col", None, None),
        P("row", "col", None, None),
        P("row", "col", None),
        P("col", None, None),
    )

    def step(params, *rest_of):
        sizes = plan(rows, cols, params.shape[1])
        part_of = list(range(cols))
        if sizes is not None:
            part_of = [part_index(sizes, r, c) for r in range(rows) for c in range(cols)]
        return jax.shard_map(
            functools.partial(body, sizes, part_of),
            mesh=mesh,
            in_specs=placed,
            out_specs=(P(), P("row", "col", None, None)),
            check_vma=False,
        )(params, *rest_of)

    return step
```

```python
import functools
import math

import jax
import jax.numpy as jnp
import ml_dtypes
import numpy as np
from jax import lax
from jax.experimental import pallas as pl
from jax.experimental.pallas import tpu as pltpu
from jax.sharding import PartitionSpec as P

decay_rate = 0.9
step_size = 0.1
LANES = 128
SUB = 8
CORES = 2
MESSAGE_ROWS = 2
EVERY = ("row", "col")
VMEM_BYTES = 48 * 1024 * 1024


def dct_table(order):
    freq = np.arange(order, dtype=np.float64)[:, None]
    place = np.arange(order, dtype=np.float64)[None, :]
    matrix = math.sqrt(2.0 / order) * np.cos(math.pi * (2.0 * place + 1.0) * freq / (2.0 * order))
    return np.where(freq == 0.0, matrix * math.sqrt(0.5), matrix)


def split_table(matrix):
    high = matrix.astype(ml_dtypes.bfloat16)
    low = (matrix - high.astype(np.float64)).astype(ml_dtypes.bfloat16)
    return np.concatenate([high, low, high], axis=1)


def product(table, field):
    high = field.astype(jnp.bfloat16)
    low = (field - high.astype(jnp.float32)).astype(jnp.bfloat16)
    stacked = jnp.concatenate([high, high, low], axis=0)
    return jnp.dot(table, stacked, preferred_element_type=jnp.float32)


def pick_kernel(width, steps, slots_of, *refs):
    sources, out_ref, held, arrived = refs[:6], refs[6], refs[7:13], refs[13]
    table_ref, chosen_ref, counts_ref, common_ref, m_ref, g_ref = held
    order, columns = m_ref.shape
    step = columns // steps
    copies = [
        pltpu.make_async_copy(source, target, arrived.at[n])
        for n, (source, target) in enumerate(zip(sources[:4], held[:4], strict=True))
    ]
    for i in range(steps):
        cut = pl.ds(i * step, step)
        for source, target in zip(sources[4:], held[4:], strict=True):
            copies.append(
                pltpu.make_async_copy(
                    source.at[0, 0, :, cut], target.at[:, cut], arrived.at[len(copies)]
                )
            )
    for copy in copies:
        copy.start()
    for copy in copies[:4]:
        copy.wait()
    chosen = chosen_ref[...]
    common = common_ref[...]
    slots = chosen.shape[0]
    slot = lax.broadcasted_iota(jnp.int32, chosen.shape, 0)
    inside = chosen == common[0:1]
    for q in range(1, common.shape[0]):
        inside = inside | (chosen == common[q : q + 1])
    live = jnp.where(slot < counts_ref[...], chosen, -1)
    rows = jnp.where(inside, live, -1)
    live = jnp.concatenate([live, live], axis=0)
    rows = jnp.concatenate([rows, rows], axis=0)
    share = width // order
    for i in range(steps):
        for copy in copies[4 + 2 * i : 6 + 2 * i]:
            copy.wait()
        for part in range(i * step // width, (i + 1) * step // width):
            cut = pl.ds(part * width, width)
            spectrum = product(table_ref[...], decay_rate * m_ref[:, cut] + g_ref[:, cut])
            for t in range(width // LANES):
                row = block_lanes(live, order, (part * width + t * LANES) // order)
                tile, within = row >> 3, row & 7
                picked = jnp.zeros((SUB, LANES), jnp.float32)
                for r in range(order // SUB):
                    here = spectrum[r * SUB : (r + 1) * SUB, t * LANES : (t + 1) * LANES]
                    here = jnp.take_along_axis(here, within, axis=0)
                    picked = jnp.where(tile == r, here, picked)
                for s in range(0, slots, MESSAGE_ROWS):
                    for to in slots_of[part]:
                        out_ref[to, :, columns_of(width, s, t * LANES)] = picked[
                            s : s + MESSAGE_ROWS
                        ]
            lanes = lax.broadcasted_iota(jnp.int32, (SUB, LANES), 1)
            each = LANES * MESSAGE_ROWS // slots
            numbers = jnp.zeros((MESSAGE_ROWS, LANES), jnp.float32)
            for s in range(0, slots, MESSAGE_ROWS):
                from_s = lanes - s // MESSAGE_ROWS * each
                from_s = part * share + jnp.clip(from_s, 0, share - 1)
                from_s = take_blocks(rows, from_s, part * share)[s : s + MESSAGE_ROWS]
                mine = lanes[:MESSAGE_ROWS] // each == s // MESSAGE_ROWS
                numbers = jnp.where(mine, from_s.astype(jnp.float32), numbers)
            for to in slots_of[part]:
                out_ref[to, :, slots // MESSAGE_ROWS * width :] = numbers


def message_shape(slots, width):
    return MESSAGE_ROWS, slots // MESSAGE_ROWS * width + LANES


def columns_of(width, slot, at):
    first = slot // MESSAGE_ROWS * width + at
    return slice(first, first + LANES)


def take_blocks(rows, lanes, first):
    base = first // LANES * LANES
    return jnp.take_along_axis(rows[:, base : base + LANES], lanes - base, axis=1)


def block_lanes(rows, order, first):
    lanes = first + lax.broadcasted_iota(jnp.int32, (SUB, LANES), 1) // order
    return take_blocks(rows, lanes, first)


def rest_kernel(skipped, start, width, slot_of, *refs):
    back_ref, chosen_ref, counts_ref, sent_ref, m_ref, g_ref, out_ref, held, gone = refs[skipped:]
    order, columns = held.shape
    chosen = chosen_ref[...]
    slots = chosen.shape[0]
    slot = lax.broadcasted_iota(jnp.int32, chosen.shape, 0)
    live = jnp.where(slot < counts_ref[...], chosen, -1)
    live = jnp.concatenate([live, live], axis=0)
    sub = lax.broadcasted_iota(jnp.int32, (SUB, LANES), 0)
    copies = []
    for part in range(columns // width):
        parts = []
        for t in range(width // LANES):
            values = [
                sent_ref[
                    slot_of[start + part],
                    s % MESSAGE_ROWS : s % MESSAGE_ROWS + 1,
                    columns_of(width, s, t * LANES),
                ]
                for s in range(slots)
            ]
            rows = block_lanes(live, order, ((start + part) * width + t * LANES) // order)
            wide = [
                (
                    jnp.broadcast_to(rows[s : s + 1], (SUB, LANES)) - sub,
                    jnp.broadcast_to(values[s], (SUB, LANES)),
                )
                for s in range(slots)
            ]
            tiles = []
            for r in range(order // SUB):
                tile = jnp.zeros((SUB, LANES), jnp.float32)
                for row, value in wide:
                    tile = jnp.where(row == r * SUB, value, tile)
                tiles.append(tile)
            parts.append(jnp.concatenate(tiles, axis=0))
        back = product(back_ref[...], jnp.concatenate(parts, axis=1))
        cut, here = pl.ds((start + part) * width, width), pl.ds(part * width, width)
        held[:, here] = decay_rate * m_ref[0, 0, :, cut] + g_ref[0, 0, :, cut] - back
        copy = pltpu.make_async_copy(held.at[:, here], out_ref.at[0, 0, :, cut], gone.at[part])
        copy.start()
        copies.append(copy)
    for copy in copies:
        copy.wait()


def part_index(sizes, row, col, xor=(0, 0, 0), core_xor=0):
    y_size, z_size, x_size, lines = sizes
    y, core = row // CORES, (row % CORES) ^ core_xor
    z, x = (col // x_size) % lines, col % x_size
    return (((y ^ xor[0]) * CORES + core) * lines + (z ^ xor[1])) * x_size + (x ^ xor[2])


def sum_kernel(sizes, back_ref, got_ref, params_ref, out_ref, held, arrived):
    order, width = out_ref.shape
    me = part_index(sizes, lax.axis_index("row"), lax.axis_index("col"))
    copy = pltpu.make_async_copy(
        params_ref.at[:, pl.ds(pl.multiple_of(me * width, LANES), width)], held, arrived
    )
    copy.start()
    lists = got_ref.shape[0]
    chunks = (got_ref.shape[2] - LANES) // width
    each = LANES // chunks
    numbers = got_ref[:, :, chunks * width :].reshape(-1, LANES)
    numbers = jnp.transpose(numbers)
    freq = lax.broadcasted_iota(jnp.int32, (order, numbers.shape[1]), 0).astype(jnp.float32)
    lane = lax.broadcasted_iota(jnp.int32, (order, LANES), 1)
    pair = LANES // order
    totals = []
    for at in range(0, width, LANES):
        table = [
            jnp.concatenate(
                [
                    (numbers[c * each + block : c * each + block + 1] == freq).astype(jnp.float32)
                    for c in range(chunks)
                ],
                axis=1,
            )
            for block in range(at // order, at // order + pair)
        ]
        table = jnp.concatenate(table, axis=0).astype(jnp.bfloat16)
        values = jnp.concatenate(
            [
                got_ref[:, :, c * width + at : c * width + at + LANES].reshape(-1, LANES)
                for c in range(chunks)
            ],
            axis=0,
        )
        high = values.astype(jnp.bfloat16)
        low = (values - high.astype(jnp.float32)).astype(jnp.bfloat16)
        total = jnp.dot(
            jnp.concatenate([table, table], axis=1),
            jnp.concatenate([high, low], axis=0),
            preferred_element_type=jnp.float32,
        )
        mine = total[:order]
        for p in range(1, pair):
            mine = jnp.where(lane // order == p, total[p * order : (p + 1) * order], mine)
        totals.append(mine)
    update = product(back_ref[...], jnp.concatenate(totals, axis=1))
    copy.wait()
    out_ref[...] = held[...] - step_size * update


def place_kernel(places, sizes, skipped, *refs):
    *pieces, out_ref, sems = refs[skipped:]
    row, col = lax.axis_index("row"), lax.axis_index("col")
    copies = []
    flat = [
        (piece.at[k] if len(piece.shape) == 3 else piece, place)
        for piece, among in zip(pieces, places, strict=True)
        for k, place in enumerate(among)
    ]
    for piece, (other, dy, dx, dz) in flat:
        width = piece.shape[-1]
        part = part_index(sizes, row, col, (dy, dz, dx), other)
        copy = pltpu.make_async_copy(
            piece,
            out_ref.at[:, pl.ds(pl.multiple_of(part * width, LANES), width)],
            sems.at[len(copies)],
        )
        copy.start()
        copies.append(copy)
    for copy in copies:
        copy.wait()


def in_hbm(array):
    return pltpu.with_memory_space_constraint(array, pltpu.HBM)


def vmem():
    return pl.BlockSpec(memory_space=pltpu.VMEM)


def limits():
    return pltpu.CompilerParams(vmem_limit_bytes=VMEM_BYTES)


def list_spec(rows, step):
    return pl.BlockSpec((rows, LANES), lambda i: (0, i * step // LANES))


def pick(forward, momentum, gradient, chosen, counts, common, part_of):
    order, columns = momentum.shape[-2:]
    parts = max(part_of) + 1
    slots_of = [[to for to, part in enumerate(part_of) if part == p] for p in range(parts)]
    width = columns // parts
    steps = min(4, parts)
    slots = chosen.shape[0]
    sources = (forward, chosen, counts, common, momentum, gradient)
    held = [pltpu.VMEM(source.shape[-2:], source.dtype) for source in sources]
    return pl.pallas_call(
        functools.partial(pick_kernel, width, steps, slots_of),
        in_specs=[pl.BlockSpec(memory_space=pltpu.HBM)] * len(sources),
        out_specs=vmem(),
        out_shape=jax.ShapeDtypeStruct((len(part_of), *message_shape(slots, width)), jnp.float32),
        scratch_shapes=held + [pltpu.SemaphoreType.DMA((4 + 2 * steps,))],
        compiler_params=limits(),
        name="pick_rows",
    )(*map(in_hbm, sources))


def rest(slot_of, back, sent, momentum, gradient, chosen, counts, first, parts, before):
    order = momentum.shape[-2]
    width = momentum.shape[-1] // len(slot_of)
    anywhere = pl.BlockSpec(memory_space=pl.ANY)
    given = [] if before is None else [before]
    return pl.pallas_call(
        functools.partial(rest_kernel, len(given), first, width, slot_of),
        in_specs=[anywhere] * len(given) + [vmem()] * 6,
        out_specs=anywhere,
        out_shape=jax.ShapeDtypeStruct(momentum.shape, jnp.float32),
        scratch_shapes=[
            pltpu.VMEM((order, parts * width), jnp.float32),
            pltpu.SemaphoreType.DMA((parts,)),
        ],
        input_output_aliases={0: 0} if given else {},
        compiler_params=limits(),
        name="residual",
        cost_estimate=pl.CostEstimate(
            flops=12 * order * order * momentum.shape[-1] * (1 if before is None else 1),
            bytes_accessed=3 * momentum.size * 4 * (1 if before is None else 1),
            transcendentals=0,
        ),
    )(*given, back, chosen, counts, sent, momentum, gradient)


def add_up(sizes, parts, back, got, params):
    order = params.shape[0]
    width = params.shape[1] // parts
    return pl.pallas_call(
        functools.partial(sum_kernel, sizes),
        in_specs=[vmem(), vmem(), pl.BlockSpec(memory_space=pltpu.HBM)],
        out_specs=vmem(),
        out_shape=jax.ShapeDtypeStruct((order, width), jnp.float32),
        scratch_shapes=[pltpu.VMEM((order, width), jnp.float32), pltpu.SemaphoreType.DMA],
        compiler_params=limits(),
        name="sum_and_update",
    )(back, got, in_hbm(params))


def spread(mine, piece, params, sizes):
    y_size, z_size, x_size, lines = sizes

    def swap(array, by):
        pairs = []
        for y in range(y_size):
            for core in range(CORES):
                for z in range(z_size):
                    for x in range(x_size):
                        here = ((y * CORES + core) * z_size + z) * x_size + x
                        there = ((y ^ by[0]) * CORES + (core ^ by[1])) * z_size + (z ^ by[2])
                        pairs.append((here, there * x_size + (x ^ by[3])))
        return lax.ppermute(array, EVERY, pairs)

    far = [(j, i) for j in range(y_size) for i in range(x_size) if j or i]
    far.sort(key=lambda at: sum(map(bool, at)))
    parts = y_size * CORES * lines * x_size
    fill = parts * 8 // 16
    line = [mine] + [swap(mine, (0, 0, j, 0)) for j in range(1, lines)]
    def mine_of(pieces):
        return [(array, [(0, *at)]) for array, *at in pieces]

    def other(pieces):
        arrays = [piece_of[0] for piece_of in pieces]
        array = arrays[0] if len(arrays) == 1 else jnp.stack(arrays)
        return (swap(array, (0, 1, 0, 0)), [(1, *piece_of[1:]) for piece_of in pieces])

    corners = [(j, i) for j, i in far if j and i]
    sides = [(j, i) for j, i in far if not (j and i)]
    near = [(own, 0, 0, n) for n, own in enumerate(line)]
    begun = [(swap(mine, (j, 0, 0, i)), j, i, 0) for j, i in corners]
    theirs = [other(near[:1])]
    held, theirs_first = lax.optimization_barrier((mine, theirs[0][0]))
    theirs = [(theirs_first, theirs[0][1])]
    gone = begun + [(swap(held, (j, 0, 0, i)), j, i, 0) for j, i in sides]
    late, done, residual = [], 0, None
    for n, own in enumerate(line[1:], 1):
        residual = piece(done, fill, residual)
        own, residual = lax.optimization_barrier((own, residual))
        done += fill
        near[n] = (own, 0, 0, n)
        late += [(swap(own, (j, 0, 0, i)), j, i, n) for j, i in sides]
        late += [(swap(array, (0, 0, n, 0)), j, i, n) for array, j, i, _ in begun]
    residual = piece(done, parts - done, residual)
    waiting = near[1:] + gone
    arrays, residual = lax.optimization_barrier(([piece_of[0] for piece_of in waiting], residual))
    waiting = [(array, *at[1:]) for array, at in zip(arrays, waiting, strict=True)]
    partial = place(mine_of(near[:1] + waiting) + theirs, sizes, params, None)
    theirs = [other(waiting[: -len(sides)]), other(waiting[-len(sides) :])]
    arrays = [piece_of[0] for piece_of in late]
    arrays, partial = lax.optimization_barrier((arrays, partial))
    late = [(array, *at[1:]) for array, at in zip(arrays, late, strict=True)]
    partial = place(mine_of(late) + theirs, sizes, params, partial)
    straight = [piece_of for piece_of in late if not (piece_of[1] and piece_of[2])]
    across = [piece_of for piece_of in late if piece_of[1] and piece_of[2]]
    partial = place([other(group) for group in (straight, across) if group], sizes, params, partial)
    return partial, residual


def place(pieces, sizes, params, partial):
    arrays = [piece[0] for piece in pieces]
    places = [piece[1] for piece in pieces]
    anywhere = pl.BlockSpec(memory_space=pl.ANY)
    given = [] if partial is None else [partial]
    return pl.pallas_call(
        functools.partial(place_kernel, places, sizes, len(given)),
        in_specs=[anywhere] * (len(given) + len(arrays)),
        out_specs=anywhere,
        out_shape=jax.ShapeDtypeStruct(params.shape, jnp.float32),
        scratch_shapes=[pltpu.SemaphoreType.DMA((sum(map(len, places)),))],
        input_output_aliases={0: 0} if given else {},
        compiler_params=limits(),
        name="place_columns",
    )(*given, *arrays)


def body(sizes, part_of, params, momentum, gradient, chosen_rows, live_counts, common_rows):
    matrix = dct_table(params.shape[0])
    forward, back = jnp.asarray(split_table(matrix)), jnp.asarray(split_table(matrix.T))
    chosen = jnp.transpose(chosen_rows[0, 0])
    counts = live_counts[0]
    common = jnp.transpose(common_rows[0])
    sent = pick(forward, momentum, gradient, chosen, counts, common, part_of)
    parts = max(part_of) + 1
    slot_of = [part_of.index(part) for part in range(parts)]
    piece = functools.partial(rest, slot_of, back, sent, momentum, gradient, chosen, counts)
    if sizes is not None:
        got = lax.all_to_all(sent, EVERY, 0, 0, tiled=True)
        mine = add_up(sizes, parts, back, got, params)
        new_params, residual = spread(mine, piece, params, sizes)
    else:
        residual = piece(0, parts, None)
        new_params = plain_update(back, sent, params)
    return new_params, residual


def plain_update(back, sent, params):
    order, columns = params.shape
    got = lax.all_to_all(sent, "col", 0, 0, tiled=True)
    got = lax.all_gather(got, "row", axis=0, tiled=True)
    width = columns // sent.shape[0]
    chunks = (got.shape[2] - LANES) // width
    values = got[:, :, : chunks * width].reshape(*got.shape[:2], chunks, width)
    numbers = got[:, :, chunks * width :].reshape(*got.shape[:2], chunks, -1)
    row = jnp.repeat(numbers[..., : width // order].astype(jnp.int32), order, axis=3)
    table = row[..., None, :] == jnp.arange(order, dtype=jnp.int32)[:, None]
    total = jnp.sum(jnp.where(table, values[..., None, :], 0.0), axis=(0, 1, 2))
    total = lax.all_gather(total, "col", axis=1, tiled=True)
    return params - step_size * product(back, total)


def plan(rows, cols, columns):
    side = rows // CORES
    depth = cols // max(side, 1)
    whole = rows == side * CORES and cols == side * depth
    if not whole or any(n < 1 or n & (n - 1) for n in (side, depth)):
        return None
    lines = max(depth // 2, 1)
    while lines > 1 and columns % (side * CORES * lines * side * LANES):
        lines //= 2
    if columns % (side * CORES * lines * side * LANES):
        return None
    return side, depth, side, lines


def solution(mesh):
    rows, cols = mesh.shape["row"], mesh.shape["col"]
    placed = (
        P(),
        P("row", "col", None, None),
        P("row", "col", None, None),
        P("row", "col", None, None),
        P("row", "col", None),
        P("col", None, None),
    )

    def step(params, *rest_of):
        sizes = plan(rows, cols, params.shape[1])
        part_of = list(range(cols))
        if sizes is not None:
            part_of = [part_index(sizes, r, c) for r in range(rows) for c in range(cols)]
        return jax.shard_map(
            functools.partial(body, sizes, part_of),
            mesh=mesh,
            in_specs=placed,
            out_specs=(P(), P("row", "col", None, None)),
            check_vma=False,
        )(params, *rest_of)

    return step
```
